32 devices in a mesh: req: 8 (over y, x, core), mlp: 4 (over z).
Axes of the slice: x: 2, y: 2, z: 4, core: 2. Of those that a mesh axis runs over, the one named last changes fastest.
Arguments:
- tokens: bfloat16 [4096, 1024], P(('req', 'mlp')), may hold values from -6 to 6
- token_owner: int32 [4096, 1], replicated, may hold values from 0 to 31; in each aligned block of 128 rows (0 to 127, 128 to 255, ...) at most 8 rows name the same one
- token_request: int32 [4096], replicated, may hold values from 0 to 3
- cache_len: int32 [128], P(('req', 'mlp')), may hold values from 1 to 512, 32768 in all
- cache_k: bfloat16 [128, 512, 1024], P(('req', 'mlp')), may hold values from -6 to 6
- cache_v: bfloat16 [128, 512, 1024], P(('req', 'mlp')), may hold values from -12 to 12
- w_qkv: bfloat16 [1024, 3072], replicated, may hold values from -0.1875 to 0.1875
- w_out: bfloat16 [1024, 1024], replicated, may hold values from -0.375 to 0.375
- w_fc1: bfloat16 [1024, 4096], P(None, 'mlp'), may hold values from -0.1875 to 0.1875
- w_fc2: bfloat16 [4096, 1024], P('mlp'), may hold values from -0.09375 to 0.09375
- ln1_gain: float32 [1024], replicated, may hold values from 0.1 to 1.9
- ln1_bias: float32 [1024], replicated, may hold values from -3 to 3
- ln2_gain: float32 [1024], replicated, may hold values from 0.1 to 1.9
- ln2_bias: float32 [1024], replicated, may hold values from -3 to 3
Outputs:
- layer_out: bfloat16 [4096, 1024], P(('req', 'mlp'))
The draws below stay inside these ranges and needn't reach their ends.
Inputs may be any that keep to these rules, and one draw needn't show every extreme that they name: `token_owner`: in each aligned block of 128 rows (the rows of one device) no owner is named more than 8 times, a bound that some block reaches; every owner is named somewhere. `cache_len`: some request has exactly 512 cached positions.
All inputs are finite; a program needn't handle non-finite values. No bound on the sum of `cache_len` on one device may be relied on, other than what follows from the above.
Results may differ from the reference program's by a relative error of at most 0.01.
Values may be sent and summed in bfloat16 or wider, within the bound.
No kernel may reach another device: no remote copies, remote signals or barrier semaphores. Data moves between devices by JAX's collectives and lax.ppermute only.
A program may use at most 128 MiB of HBM per device.

```python
import math
import jax
import jax.numpy as jnp
import numpy as np
from jax import lax

D = 1024
HEADS = 16
FF = 4096
TOK_DEV = 128
REQS = 4
CTX = 512
CAP = 8
TOKENS = 4096
OWNED = 128
N_REQ = 8
N_MLP = 4
DEVICES = 32


def set_ends(drawn, stream_key, least, largest):
    place = [jax.random.randint(jax.random.fold_in(stream_key, axis), (), 0, length) for axis, length in enumerate(drawn.shape)]
    longest = drawn.shape.index(max(drawn.shape))
    neighbour = place[:longest] + [(place[longest] + 1) % drawn.shape[longest]] + place[longest + 1:]
    return drawn.at[tuple(place)].set(least).at[tuple(neighbour)].set(largest)


def shard_levels(own_key, extent, split, least, top_value):
    factor_of = 1.0
    for position, blocks in split:
        steps = jax.random.uniform(jax.random.fold_in(jax.random.fold_in(own_key, 6), position), (blocks,), jnp.float32, least / len(split), top_value / len(split))
        factor_of = factor_of * jnp.repeat(jnp.exp(steps), extent[position] // blocks).reshape((-1,) + (1,) * (len(extent) - 1 - position))
    return factor_of


def profile(number_of, total, limit, lean):
    loads = [(1 << 20) // math.isqrt(grade ** lean) + 1 for grade in range(2, number_of + 1)]
    surplus, counts = total - limit - (number_of - 1), [1] * (number_of - 1)
    while surplus > 0:
        free = [i for i in range(number_of - 1) if counts[i] < limit]
        pool, budget = sum([loads[i] for i in free]), surplus
        for i in free:
            addition = min(limit - counts[i], max(1, budget * loads[i] // pool), surplus)
            counts[i] = counts[i] + addition
            surplus = surplus - addition
    return np.array([limit] + counts)


def ragged(rng, number_of, total, reach, lean):
    if number_of == 2:
        one = jax.random.randint(rng, (), max(1, total - reach), min(reach, total - 1) + 1)
        return jnp.stack([one, total - one])
    sizes = jnp.asarray(profile(number_of, total, reach, lean), jnp.int32)
    pairs = (number_of - 1) // 2
    donor, taker = sizes[1:1 + 2 * pairs:2], sizes[2:2 + 2 * pairs:2]
    room = jnp.minimum(donor - 1, reach - taker)
    moved = jax.random.randint(jax.random.fold_in(rng, 1), (pairs,), 0, 1 << 20) % (room + 1)
    sizes = sizes.at[1:1 + 2 * pairs:2].set(donor - moved).at[2:2 + 2 * pairs:2].set(taker + moved)
    return sizes[jax.random.permutation(jax.random.fold_in(rng, 2), number_of)]


def shared_out(own_key, own, number, rows, count, top, bound, slope):
    order = jax.random.permutation(own_key, count)
    crowded, ordinary = load_shares(count, rows * top, bound, slope, True), load_shares(count, rows * top, bound, slope, False)
    places = jnp.arange(count)

    def named(sizes, turn):
        used = int((sizes > 0).sum())
        fixed = max(1, used // 4)
        passed = fixed + (places - fixed + turn * (used - fixed)) % max(1, count - fixed)
        return jnp.zeros((count,), jnp.int32).at[order[jnp.where(places < fixed, places, passed)]].set(jnp.asarray(sizes, jnp.int32))

    sizes = jnp.where(number % 4 == 0, named(crowded, number // 4), named(ordinary, number - number // 4 - 1))
    mixed = jax.random.permutation(jax.random.fold_in(own, 3), count)
    source_of, taker = mixed[0:count // 2 * 2:2], mixed[1:count // 2 * 2:2]
    margin = jnp.minimum(sizes[source_of] - 1, bound - sizes[taker]) // 2
    margin = jnp.where((source_of == order[0]) | (taker == order[0]) | (sizes[taker] == 0), 0, jnp.maximum(margin, 0))
    passed = jax.random.randint(jax.random.fold_in(own, 4), (count // 2,), 0, 1 << 20) % (margin + 1)
    sizes = sizes.at[source_of].add(-passed).at[taker].add(passed)
    labels = jnp.searchsorted(jnp.cumsum(sizes), jnp.arange(rows * top), side="right").astype(jnp.int32)
    table = labels.reshape(top, rows).T
    table = table[jax.random.permutation(jax.random.fold_in(own, 1), rows)]
    turn = jax.random.randint(jax.random.fold_in(own, 2), (rows, 1), 0, top)
    return jnp.take_along_axis(table, (jnp.arange(top)[None, :] + turn) % top, axis=1)


def load_shares(amount, total, limit, slope, full):
    weights = [(1 << 20) // math.isqrt(grade ** slope) + 1 for grade in range(1, amount + 1)]
    largest = limit if full else min(limit, max(-(-total // amount), total * weights[0] // sum(weights)))
    least = 1 if total - largest >= amount - 1 else 0
    given, surplus = [largest] + [least] * (amount - 1), total - largest - least * (amount - 1)
    while surplus > 0:
        free = [i for i in range(1, amount) if given[i] < largest] or [i for i in range(1, amount) if given[i] < limit]
        pool, budget = sum([weights[i] for i in free]), surplus
        for i in free:
            extra = min(limit - given[i], max(1, budget * weights[i] // pool), surplus)
            given[i] = given[i] + extra
            surplus = surplus - extra
    return np.array(given)


def normal_values(key, shape, scale, reach, cuts=(), held_as=jnp.bfloat16):
    entries = scale * jax.random.normal(key, shape, jnp.float32)
    if cuts:
        entries = entries * shard_levels(key, shape, cuts, -0.22, 0.18)
    return jnp.clip(entries, -reach, reach).astype(held_as)


def setup_inputs(seed: int = 0) -> dict:
    key_of = jax.random.split(jax.random.key(seed), 15)
    tokens = normal_values(key_of[0], (TOKENS, D), 1.0, 6.0, ((0, 32),))
    token_owner_keys = jax.random.split(jax.random.fold_in(key_of[1], 1), TOKENS // TOK_DEV)
    token_owner_turns = jax.random.permutation(jax.random.fold_in(key_of[1], 3), TOKENS // TOK_DEV)
    token_owner = jax.vmap(lambda own, number: shared_out(jax.random.fold_in(key_of[1], 2), own, number, TOK_DEV, DEVICES, 1, CAP, 1))(token_owner_keys, token_owner_turns).reshape((TOKENS, 1))
    token_request = set_ends(jax.random.randint(key_of[2], (TOKENS,), 0, REQS), jax.random.fold_in(key_of[2], 1), 0, REQS - 1).astype(jnp.int32)
    cache_len = ragged(key_of[3], OWNED, OWNED * CTX // 2, CTX, 1).astype(jnp.int32)
    cache_k = normal_values(key_of[4], (OWNED, CTX, D), 1.0, 6.0, ((0, 32),))
    cache_v = normal_values(key_of[5], (OWNED, CTX, D), 2.0, 12.0, ((0, 32),))
    w_qkv = normal_values(key_of[6], (D, 3 * D), D ** -0.5, 0.1875)
    w_out = normal_values(key_of[7], (D, D), (D // 4) ** -0.5, 0.375)
    w_fc1 = normal_values(key_of[8], (D, FF), D ** -0.5, 0.1875, ((1, 4),))
    w_fc2 = normal_values(key_of[9], (FF, D), FF ** -0.5, 0.09375, ((0, 4),))
    ln1_gain = jnp.clip(1.0 + 0.18 * jax.random.normal(key_of[10], (D,), jnp.float32), 0.1, 1.9)
    ln1_bias = normal_values(key_of[11], (D,), 0.5, 3.0, (), jnp.float32)
    ln2_gain = jnp.clip(1.0 + 0.18 * jax.random.normal(key_of[12], (D,), jnp.float32), 0.1, 1.9)
    ln2_bias = normal_values(key_of[13], (D,), 0.5, 3.0, (), jnp.float32)
    return dict(tokens=tokens, token_owner=token_owner, token_request=token_request, cache_len=cache_len, cache_k=cache_k, cache_v=cache_v, w_qkv=w_qkv, w_out=w_out, w_fc1=w_fc1, w_fc2=w_fc2, ln1_gain=ln1_gain, ln1_bias=ln1_bias, ln2_gain=ln2_gain, ln2_bias=ln2_bias)


epsilon = 1e-05

def layer_norm(values, gain, shift):
    center = values - lax.optimization_barrier(jnp.mean(values, axis=-1, keepdims=True))
    spread = lax.optimization_barrier(jnp.mean(center * center, axis=-1, keepdims=True))
    return center * lax.rsqrt(spread + epsilon) * gain + shift

def slot_table(owners_flat, requests_flat, owner_index, devices, tok_dev, capacity):
    owners = owners_flat.reshape(devices, tok_dev)
    requests = requests_flat.reshape(devices, tok_dev)
    mine_mask = (owners == owner_index).astype(jnp.int32)
    ranking = (jnp.cumsum(mine_mask, axis=1) - 1).astype(jnp.int32)
    places = jnp.arange(capacity, dtype=jnp.int32)
    hit_table = mine_mask[:, :, None] * (ranking[:, :, None] == places[None, None, :]).astype(jnp.int32)
    filled = lax.optimization_barrier(jnp.sum(hit_table, axis=1)).astype(jnp.int32)
    positions = jnp.arange(tok_dev, dtype=jnp.int32)
    local_row = lax.optimization_barrier(jnp.sum(hit_table * positions[None, :, None], axis=1)).astype(jnp.int32)
    sources = jnp.arange(devices, dtype=jnp.int32)[:, None]
    global_row = jnp.where(filled > 0, sources * tok_dev + local_row, -1).astype(jnp.int32).reshape(-1)
    slot_request = lax.optimization_barrier(jnp.sum(hit_table * requests[:, :, None], axis=1)).astype(jnp.int32).reshape(-1)
    return (global_row, slot_request, filled.reshape(-1))

def attend(projections, cache_keys, cache_values, lengths, global_row, slot_request, filled):
    slot_count = projections.shape[0]
    width = projections.shape[1] // 3
    head_dim = width // HEADS
    score_scale = head_dim ** (-0.5)
    queries = projections[:, :width].reshape(slot_count, HEADS, head_dim).astype(jnp.float32)
    key_new = projections[:, width:2 * width].reshape(slot_count, HEADS, head_dim).astype(jnp.float32)
    value_new = projections[:, 2 * width:].reshape(slot_count, HEADS, head_dim).astype(jnp.float32)
    key_old = cache_keys.reshape(REQS * CTX, HEADS, head_dim).astype(jnp.float32)
    value_old = cache_values.reshape(REQS * CTX, HEADS, head_dim).astype(jnp.float32)
    key_owner = jnp.arange(REQS * CTX, dtype=jnp.int32) // CTX
    key_place = jnp.arange(REQS * CTX, dtype=jnp.int32) % CTX
    key_limit = jnp.repeat(lengths, CTX)
    old_mask = (key_owner[None, :] == slot_request[:, None]) & (key_place[None, :] < key_limit[None, :])
    new_mask = (filled[None, :] > 0) & (slot_request[None, :] == slot_request[:, None]) & (global_row[None, :] <= global_row[:, None])
    old_score = jnp.einsum('rhd,khd->hrk', queries, key_old) * score_scale
    new_score = jnp.einsum('rhd,shd->hrs', queries, key_new) * score_scale
    old_exp = jnp.where(old_mask[None], jnp.exp(old_score), jnp.float32(0.0))
    new_exp = jnp.where(new_mask[None], jnp.exp(new_score), jnp.float32(0.0))
    denominator = lax.optimization_barrier(jnp.sum(old_exp, axis=-1)) + lax.optimization_barrier(jnp.sum(new_exp, axis=-1))
    old_weight = (old_exp / denominator[:, :, None]).astype(jnp.bfloat16)
    new_weight = (new_exp / denominator[:, :, None]).astype(jnp.bfloat16)
    result = jnp.einsum('hrk,khd->rhd', old_weight.astype(jnp.float32), value_old)
    result = result + jnp.einsum('hrs,shd->rhd', new_weight.astype(jnp.float32), value_new)
    return result.reshape(slot_count, width).astype(jnp.bfloat16)

def reference(tokens, token_owner, token_request, cache_len, cache_k, cache_v, w_qkv, w_out, w_fc1, w_fc2, ln1_gain, ln1_bias, ln2_gain, ln2_bias):
    devices = N_REQ * N_MLP
    projections = jnp.dot(tokens, w_qkv, preferred_element_type=jnp.float32).astype(jnp.bfloat16)
    owners_flat = token_owner.reshape(-1)

    def one_owner(owner_index):
        global_row, slot_request, filled = slot_table(owners_flat, token_request, owner_index, devices, TOK_DEV, CAP)
        picked = projections[jnp.maximum(global_row, 0)]
        lengths = lax.dynamic_slice_in_dim(cache_len, owner_index * REQS, REQS)
        keys_here = lax.dynamic_slice_in_dim(cache_k, owner_index * REQS, REQS)
        values_here = lax.dynamic_slice_in_dim(cache_v, owner_index * REQS, REQS)
        return (attend(picked, keys_here, values_here, lengths, global_row, slot_request, filled), global_row)
    attended, row_index = lax.map(one_owner, jnp.arange(devices, dtype=jnp.int32))
    target = jnp.where(row_index >= 0, row_index, TOKENS).astype(jnp.int32).reshape(-1)
    attn_rows = jnp.zeros((TOKENS, D), jnp.bfloat16).at[target].set(attended.reshape(-1, D), mode='drop')
    normed = layer_norm(jnp.dot(attn_rows, w_out, preferred_element_type=jnp.float32) + tokens.astype(jnp.float32), ln1_gain, ln1_bias).astype(jnp.bfloat16)
    hidden = jax.nn.gelu(jnp.dot(normed, w_fc1, preferred_element_type=jnp.float32), approximate=False).astype(jnp.bfloat16)
    summed = jnp.dot(hidden, w_fc2, preferred_element_type=jnp.float32)
    return layer_norm(normed.astype(jnp.float32) + summed, ln2_gain, ln2_bias).astype(jnp.bfloat16)
```

```python
import functools

import jax
import jax.numpy as jnp
from jax import lax
from jax.experimental import pallas as pl
from jax.experimental.pallas import tpu as pltpu
from jax.sharding import PartitionSpec as P

HEADS = 16
GROUP = 4
TILE = 64
MASKED = -1e30
VMEM_LIMIT = 56 * 1024 * 1024

epsilon = 1e-05


def layer_norm(values, gain, shift):
    center = values - jnp.mean(values, axis=-1, keepdims=True)
    spread = jnp.mean(center * center, axis=-1, keepdims=True)
    return center * lax.rsqrt(spread + epsilon) * gain + shift


def iota(shape, dim):
    return lax.broadcasted_iota(jnp.int32, shape, dim)


def own_pairs(owners_ref, me):
    tok_dev = owners_ref.shape[1]
    across = jnp.broadcast_to(owners_ref[pl.ds(me, 1), :], (tok_dev, tok_dev)).astype(jnp.float32)
    return across, across.T


def dispatch_kernel(capacity, me_ref, owners_ref, tokens_ref, out_ref):
    tok_dev = tokens_ref.shape[0]
    slots = out_ref.shape[0]
    across, down = own_pairs(owners_ref, me_ref[0])
    square = (tok_dev, tok_dev)
    earlier = (across == down) & (iota(square, 0) < iota(square, 1))
    rank = jnp.sum(jnp.where(earlier, 1.0, 0.0), axis=0, keepdims=True)
    column = across[:1, :] * capacity + rank
    onehot = iota((slots, tok_dev), 0).astype(jnp.float32) == column
    onehot = jnp.where(onehot, 1.0, 0.0).astype(jnp.bfloat16)
    out_ref[...] = jnp.dot(
        onehot, tokens_ref[...], preferred_element_type=jnp.float32
    ).astype(jnp.bfloat16)


def table_kernel(
    capacity, me_ref, owners_ref, requests_ref, back_ref, sort_ref, unsort_ref, starts_ref
):
    devices, tok_dev = owners_ref.shape
    slots = sort_ref.shape[0]
    me = me_ref[0]
    across, down = own_pairs(owners_ref, me)
    square = (tok_dev, tok_dev)
    earlier = (across == down) & (iota(square, 1) < iota(square, 0))
    rank = jnp.sum(jnp.where(earlier, 1.0, 0.0), axis=1, keepdims=True)
    column = down[:, :1] * capacity + rank
    back = iota((tok_dev, slots), 1).astype(jnp.float32) == column
    back_ref[...] = jnp.where(back, 1.0, 0.0).astype(jnp.bfloat16)
    mine = owners_ref[...] == me
    before = jnp.where(iota(square, 0) < iota(square, 1), 1.0, 0.0).astype(jnp.bfloat16)
    ranking = jnp.dot(
        jnp.where(mine, 1.0, 0.0).astype(jnp.bfloat16), before, preferred_element_type=jnp.float32
    ).astype(jnp.bfloat16)
    coded = jnp.where(mine, requests_ref[...] + 1, 0).astype(jnp.float32).astype(jnp.bfloat16)
    slot = iota((slots, devices), 0)
    source = iota((slots, devices), 1)
    from_here = (slot >= source * capacity) & (slot < (source + 1) * capacity)
    place = jnp.sum(jnp.where(from_here, slot - source * capacity, 0), axis=1, keepdims=True)
    from_here = jnp.where(from_here, 1.0, 0.0).astype(jnp.bfloat16)
    rank_of = jnp.dot(from_here, ranking, preferred_element_type=jnp.float32)
    code_of = jnp.dot(from_here, coded, preferred_element_type=jnp.float32)
    hit = rank_of == place.astype(jnp.float32)
    code = jnp.sum(jnp.where(hit, code_of, 0.0), axis=1, keepdims=True)
    wide = (slots, slots)
    code_i = jnp.broadcast_to(code, wide)
    code_j = code_i.T
    sub, lane = iota(wide, 0), iota(wide, 1)
    ahead_j = (code_j > 0) & ((code_j < code_i) | ((code_j == code_i) & (lane < sub)))
    ahead_i = (code_i > 0) & ((code_i < code_j) | ((code_i == code_j) & (sub < lane)))
    place_i = jnp.sum(jnp.where(ahead_j, 1.0, 0.0), axis=1, keepdims=True)
    place_j = jnp.sum(jnp.where(ahead_i, 1.0, 0.0), axis=0, keepdims=True)
    sort = (place_j == sub.astype(jnp.float32)) & (code_j > 0)
    unsort = (place_i == lane.astype(jnp.float32)) & (code_i > 0)
    sort_ref[...] = jnp.where(sort, 1.0, 0.0).astype(jnp.bfloat16)
    unsort_ref[...] = jnp.where(unsort, 1.0, 0.0).astype(jnp.bfloat16)
    few = code_j[:8, :]
    upto = (few > 0) & (few <= iota((8, slots), 0).astype(jnp.float32))
    starts = jnp.sum(jnp.where(upto, 1.0, 0.0), axis=1, keepdims=True)
    starts_ref[...] = jnp.broadcast_to(starts, starts_ref.shape).astype(jnp.int32)


def attend_kernel(
    starts_ref,
    lengths_ref,
    sort_ref,
    unsort_ref,
    x_ref,
    w_ref,
    keys_ref,
    values_ref,
    out_ref,
    sorted_ref,
    proj_ref,
    att_ref,
):
    slots, width = x_ref.shape
    requests, context, _ = keys_ref.shape
    head_dim = width // HEADS
    span = GROUP * head_dim
    scale = head_dim ** (-0.5)
    sorted_ref[...] = jnp.dot(
        sort_ref[...], x_ref[...], preferred_element_type=jnp.float32
    ).astype(jnp.bfloat16)
    att_ref[...] = jnp.zeros_like(att_ref)

    @pl.loop(0, 3 * width // span)
    def _(c):
        columns = pl.ds(pl.multiple_of(c * span, span), span)
        proj_ref[:, columns] = jnp.dot(
            sorted_ref[...], w_ref[:, columns], preferred_element_type=jnp.float32
        ).astype(jnp.bfloat16)

    starts = [starts_ref[r, 0] for r in range(requests + 1)]
    filled = starts[requests]

    @pl.loop(0, pl.cdiv(filled, TILE))
    def _(t):
        first = pl.multiple_of(t * TILE, TILE)
        rows = pl.ds(first, TILE)
        last = jnp.minimum(first + TILE, filled) - 1
        low = sum((starts[r] <= first).astype(jnp.int32) for r in range(1, requests))
        high = sum((starts[r] <= last).astype(jnp.int32) for r in range(1, requests))

        @pl.loop(low, high + 1)
        def _(r):
            begin, end = starts_ref[r, 0], starts_ref[r + 1, 0]

            @pl.when(end > begin)
            def _():
                row = iota((TILE, 1), 0) + first
                in_request = (row >= begin) & (row < end)
                key = iota((1, slots), 1)
                seen = (key >= begin) & (key <= row)
                new_bias = jnp.where(seen, 0.0, MASKED)
                new_bias = jnp.concatenate([new_bias] * GROUP, axis=0)
                valid = iota((1, context), 1) < lengths_ref[r]
                old_bias = jnp.where(valid, 0.0, MASKED)
                head_of = iota((1, span), 1) // head_dim
                for g in range(HEADS // GROUP):
                    lo = g * span
                    q = proj_ref[rows, lo : lo + span]
                    q = jnp.concatenate(
                        [jnp.where(head_of == h, q, jnp.bfloat16(0)) for h in range(GROUP)], axis=0
                    )
                    k_new = proj_ref[:, width + lo : width + lo + span]
                    v_new = proj_ref[:, 2 * width + lo : 2 * width + lo + span]
                    k_old = keys_ref[r, :, lo : lo + span]
                    v_old = values_ref[r, :, lo : lo + span]
                    across = (((1,), (1,)), ((), ()))
                    s_old = (
                        lax.dot_general(q, k_old, across, preferred_element_type=jnp.float32)
                        * scale
                        + old_bias
                    )
                    s_new = (
                        lax.dot_general(q, k_new, across, preferred_element_type=jnp.float32)
                        * scale
                        + new_bias
                    )
                    top = jnp.maximum(
                        jnp.max(s_old, axis=1, keepdims=True), jnp.max(s_new, axis=1, keepdims=True)
                    )
                    p_old = jnp.exp(s_old - top)
                    p_new = jnp.exp(s_new - top)
                    total = jnp.sum(p_old, axis=1, keepdims=True) + jnp.sum(
                        p_new, axis=1, keepdims=True
                    )
                    part = jnp.dot(
                        p_old.astype(jnp.bfloat16), v_old, preferred_element_type=jnp.float32
                    )
                    part += jnp.dot(
                        p_new.astype(jnp.bfloat16), v_new, preferred_element_type=jnp.float32
                    )
                    part = part / total
                    mixed = jnp.zeros((TILE, span), jnp.float32)
                    for h in range(GROUP):
                        mixed = jnp.where(head_of == h, part[h * TILE : (h + 1) * TILE], mixed)
                    kept = att_ref[rows, lo : lo + span]
                    att_ref[rows, lo : lo + span] = jnp.where(
                        in_request, mixed.astype(jnp.bfloat16), kept
                    )

    out_ref[...] = jnp.dot(
        unsort_ref[...], att_ref[...], preferred_element_type=jnp.float32
    ).astype(jnp.bfloat16)


def vmem(n):
    return [pl.BlockSpec(memory_space=pltpu.VMEM)] * n


def smem(n):
    return [pl.BlockSpec(memory_space=pltpu.SMEM)] * n


def params(limit=VMEM_LIMIT):
    return pltpu.CompilerParams(vmem_limit_bytes=limit)


def shape(dims, dtype=jnp.bfloat16):
    return jax.ShapeDtypeStruct(dims, dtype)


def per_device(
    tokens,
    token_owner,
    token_request,
    cache_len,
    cache_k,
    cache_v,
    w_qkv,
    w_out,
    w_fc1,
    w_fc2,
    ln1_gain,
    ln1_bias,
    ln2_gain,
    ln2_bias,
):
    n_req = lax.axis_size("req")
    n_mlp = lax.axis_size("mlp")
    devices = n_req * n_mlp
    owner_index = lax.axis_index("req") * n_mlp + lax.axis_index("mlp")
    tok_dev, width = tokens.shape
    capacity = max(2, 2 * tok_dev // devices)
    slots = devices * capacity
    me = owner_index.astype(jnp.int32).reshape(1)
    owners = token_owner.reshape(devices, tok_dev)
    requests = token_request.reshape(devices, tok_dev)
    outgoing = pl.pallas_call(
        functools.partial(dispatch_kernel, capacity),
        out_shape=shape((slots, width)),
        in_specs=smem(1) + vmem(2),
        out_specs=vmem(1)[0],
        compiler_params=params(16 * 1024 * 1024),
        name="dispatch",
    )(me, owners, tokens)
    arrived = lax.all_to_all(
        outgoing.reshape(devices, capacity, width),
        ("req", "mlp"),
        split_axis=0,
        concat_axis=0,
        tiled=True,
    )
    back, sort, unsort, starts = pl.pallas_call(
        functools.partial(table_kernel, capacity),
        out_shape=(
            shape((tok_dev, slots)),
            shape((slots, slots)),
            shape((slots, slots)),
            shape((8, 128), jnp.int32),
        ),
        in_specs=smem(1) + vmem(2),
        out_specs=tuple(vmem(4)),
        compiler_params=params(16 * 1024 * 1024),
        cost_estimate=pl.CostEstimate(flops=40_000_000, bytes_accessed=400_000, transcendentals=0),
        name="table",
    )(me, owners, requests)
    attended = pl.pallas_call(
        attend_kernel,
        out_shape=shape((slots, width)),
        in_specs=smem(2) + vmem(6),
        out_specs=vmem(1)[0],
        scratch_shapes=[
            pltpu.VMEM((slots, width), jnp.bfloat16),
            pltpu.VMEM((slots, 3 * width), jnp.bfloat16),
            pltpu.VMEM((slots, width), jnp.bfloat16),
        ],
        compiler_params=params(),
        name="attend",
    )(
        starts,
        cache_len,
        sort,
        unsort,
        arrived.reshape(slots, width),
        w_qkv,
        cache_k,
        cache_v,
    )
    returned = lax.all_to_all(
        attended.reshape(devices, capacity, width),
        ("req", "mlp"),
        split_axis=0,
        concat_axis=0,
        tiled=True,
    )
    attn_rows = jnp.dot(
        back, returned.reshape(slots, width), preferred_element_type=jnp.float32
    ).astype(jnp.bfloat16)
    projected_out = jnp.dot(attn_rows, w_out, preferred_element_type=jnp.float32)
    normed = layer_norm(projected_out + tokens.astype(jnp.float32), ln1_gain, ln1_bias).astype(
        jnp.bfloat16
    )
    gathered = lax.all_gather(normed, "mlp", axis=0, tiled=True)
    hidden = jax.nn.gelu(
        jnp.dot(gathered, w_fc1, preferred_element_type=jnp.float32), approximate=False
    ).astype(jnp.bfloat16)
    summed = lax.psum_scatter(
        jnp.dot(hidden, w_fc2, preferred_element_type=jnp.float32).astype(jnp.bfloat16),
        "mlp",
        scatter_dimension=0,
        tiled=True,
    ).astype(jnp.float32)
    return layer_norm(normed.astype(jnp.float32) + summed, ln2_gain, ln2_bias).astype(jnp.bfloat16)


def solution(mesh):
    placed = (
        P(("req", "mlp"), None),
        P(),
        P(),
        P(("req", "mlp")),
        P(("req", "mlp"), None, None),
        P(("req", "mlp"), None, None),
        P(),
        P(),
        P(None, "mlp"),
        P("mlp", None),
        P(),
        P(),
        P(),
        P(),
    )
    return jax.shard_map(
        per_device, mesh=mesh, in_specs=placed, out_specs=P(("req", "mlp"), None), check_vma=False
    )
```

```python
import functools

import jax
import jax.numpy as jnp
from jax import lax
from jax.experimental import pallas as pl
from jax.experimental.pallas import tpu as pltpu
from jax.sharding import PartitionSpec as P

HEADS = 16
GROUP = 4
TILE = 64
MASKED = -1e30
VMEM_LIMIT = 56 * 1024 * 1024

ALL = ("req", "other", "pair")

epsilon = 1e-05


def layer_norm(values, gain, shift):
    center = values - jnp.mean(values, axis=-1, keepdims=True)
    spread = jnp.mean(center * center, axis=-1, keepdims=True)
    return center * lax.rsqrt(spread + epsilon) * gain + shift


def iota(shape, dim):
    return lax.broadcasted_iota(jnp.int32, shape, dim)


def own_pairs(owners_ref, me):
    tok_dev = owners_ref.shape[1]
    across = jnp.broadcast_to(owners_ref[pl.ds(me, 1), :], (tok_dev, tok_dev)).astype(jnp.float32)
    return across, across.T


def dispatch_kernel(capacity, me_ref, owners_ref, tokens_ref, out_ref):
    tok_dev = tokens_ref.shape[0]
    slots = out_ref.shape[0]
    across, down = own_pairs(owners_ref, me_ref[0])
    square = (tok_dev, tok_dev)
    earlier = (across == down) & (iota(square, 0) < iota(square, 1))
    rank = jnp.sum(jnp.where(earlier, 1.0, 0.0), axis=0, keepdims=True)
    column = across[:1, :] * capacity + rank
    onehot = iota((slots, tok_dev), 0).astype(jnp.float32) == column
    onehot = jnp.where(onehot, 1.0, 0.0).astype(jnp.bfloat16)
    out_ref[...] = jnp.dot(
        onehot, tokens_ref[...], preferred_element_type=jnp.float32
    ).astype(jnp.bfloat16)


def table_kernel(
    capacity, me_ref, owners_ref, requests_ref, back_ref, sort_ref, unsort_ref, starts_ref
):
    devices, tok_dev = owners_ref.shape
    slots = sort_ref.shape[0]
    me = me_ref[0]
    across, down = own_pairs(owners_ref, me)
    square = (tok_dev, tok_dev)
    earlier = (across == down) & (iota(square, 1) < iota(square, 0))
    rank = jnp.sum(jnp.where(earlier, 1.0, 0.0), axis=1, keepdims=True)
    column = down[:, :1] * capacity + rank
    back = iota((tok_dev, slots), 1).astype(jnp.float32) == column
    back_ref[...] = jnp.where(back, 1.0, 0.0).astype(jnp.bfloat16)
    mine = owners_ref[...] == me
    before = jnp.where(iota(square, 0) < iota(square, 1), 1.0, 0.0).astype(jnp.bfloat16)
    ranking = jnp.dot(
        jnp.where(mine, 1.0, 0.0).astype(jnp.bfloat16), before, preferred_element_type=jnp.float32
    ).astype(jnp.bfloat16)
    coded = jnp.where(mine, requests_ref[...] + 1, 0).astype(jnp.float32).astype(jnp.bfloat16)
    slot = iota((slots, devices), 0)
    source = iota((slots, devices), 1)
    from_here = (slot >= source * capacity) & (slot < (source + 1) * capacity)
    place = jnp.sum(jnp.where(from_here, slot - source * capacity, 0), axis=1, keepdims=True)
    from_here = jnp.where(from_here, 1.0, 0.0).astype(jnp.bfloat16)
    rank_of = jnp.dot(from_here, ranking, preferred_element_type=jnp.float32)
    code_of = jnp.dot(from_here, coded, preferred_element_type=jnp.float32)
    hit = rank_of == place.astype(jnp.float32)
    code = jnp.sum(jnp.where(hit, code_of, 0.0), axis=1, keepdims=True)
    wide = (slots, slots)
    code_i = jnp.broadcast_to(code, wide)
    code_j = code_i.T
    sub, lane = iota(wide, 0), iota(wide, 1)
    ahead_j = (code_j > 0) & ((code_j < code_i) | ((code_j == code_i) & (lane < sub)))
    ahead_i = (code_i > 0) & ((code_i < code_j) | ((code_i == code_j) & (sub < lane)))
    place_i = jnp.sum(jnp.where(ahead_j, 1.0, 0.0), axis=1, keepdims=True)
    place_j = jnp.sum(jnp.where(ahead_i, 1.0, 0.0), axis=0, keepdims=True)
    sort = (place_j == sub.astype(jnp.float32)) & (code_j > 0)
    unsort = (place_i == lane.astype(jnp.float32)) & (code_i > 0)
    sort_ref[...] = jnp.where(sort, 1.0, 0.0).astype(jnp.bfloat16)
    unsort_ref[...] = jnp.where(unsort, 1.0, 0.0).astype(jnp.bfloat16)
    few = code_j[:8, :]
    upto = (few > 0) & (few <= iota((8, slots), 0).astype(jnp.float32))
    starts = jnp.sum(jnp.where(upto, 1.0, 0.0), axis=1, keepdims=True)
    starts_ref[...] = jnp.broadcast_to(starts, starts_ref.shape).astype(jnp.int32)


def attend_kernel(
    starts_ref,
    lengths_ref,
    sort_ref,
    unsort_ref,
    x_ref,
    w_ref,
    keys_ref,
    values_ref,
    out_ref,
    sorted_ref,
    proj_ref,
    att_ref,
    w_held,
    keys_held,
    values_held,
    sems,
):
    slots, width = x_ref.shape
    requests, context, _ = keys_ref.shape
    head_dim = width // HEADS
    span = GROUP * head_dim
    scale = head_dim ** (-0.5)
    loads = [
        pltpu.make_async_copy(
            w_ref.at[:, i * width : (i + 1) * width],
            w_held.at[:, i * width : (i + 1) * width],
            sems.at[i],
        )
        for i in range(3)
    ]
    loads.append(pltpu.make_async_copy(keys_ref, keys_held, sems.at[3]))
    loads.append(pltpu.make_async_copy(values_ref, values_held, sems.at[4]))
    for load in loads:
        load.start()
    sorted_ref[...] = jnp.dot(
        sort_ref[...], x_ref[...], preferred_element_type=jnp.float32
    ).astype(jnp.bfloat16)
    att_ref[...] = jnp.zeros_like(att_ref)

    for i in range(3):
        loads[i].wait()

        @pl.loop(0, width // span)
        def _(c):
            columns = pl.ds(pl.multiple_of(i * width + c * span, span), span)
            proj_ref[:, columns] = jnp.dot(
                sorted_ref[...], w_held[:, columns], preferred_element_type=jnp.float32
            ).astype(jnp.bfloat16)

    loads[3].wait()
    loads[4].wait()
    starts = [starts_ref[r, 0] for r in range(requests + 1)]
    filled = starts[requests]

    @pl.loop(0, pl.cdiv(filled, TILE))
    def _(t):
        first = pl.multiple_of(t * TILE, TILE)
        rows = pl.ds(first, TILE)
        last = jnp.minimum(first + TILE, filled) - 1
        low = sum((starts[r] <= first).astype(jnp.int32) for r in range(1, requests))
        high = sum((starts[r] <= last).astype(jnp.int32) for r in range(1, requests))

        @pl.loop(low, high + 1)
        def _(r):
            begin, end = starts_ref[r, 0], starts_ref[r + 1, 0]

            @pl.when(end > begin)
            def _():
                row = iota((TILE, 1), 0) + first
                in_request = (row >= begin) & (row < end)
                key = iota((1, slots), 1)
                seen = (key >= begin) & (key <= row)
                new_bias = jnp.where(seen, 0.0, MASKED)
                new_bias = jnp.concatenate([new_bias] * GROUP, axis=0)
                valid = iota((1, context), 1) < lengths_ref[r]
                old_bias = jnp.where(valid, 0.0, MASKED)
                head_of = iota((1, span), 1) // head_dim
                for g in range(HEADS // GROUP):
                    lo = g * span
                    q = proj_ref[rows, lo : lo + span]
                    q = jnp.concatenate(
                        [jnp.where(head_of == h, q, jnp.bfloat16(0)) for h in range(GROUP)], axis=0
                    )
                    k_new = proj_ref[:, width + lo : width + lo + span]
                    v_new = proj_ref[:, 2 * width + lo : 2 * width + lo + span]
                    k_old = keys_held[r, :, lo : lo + span]
                    v_old = values_held[r, :, lo : lo + span]
                    across = (((1,), (1,)), ((), ()))
                    s_old = (
                        lax.dot_general(q, k_old, across, preferred_element_type=jnp.float32)
                        * scale
                        + old_bias
                    )
                    s_new = (
                        lax.dot_general(q, k_new, across, preferred_element_type=jnp.float32)
                        * scale
                        + new_bias
                    )
                    top = jnp.maximum(
                        jnp.max(s_old, axis=1, keepdims=True), jnp.max(s_new, axis=1, keepdims=True)
                    )
                    p_old = jnp.exp(s_old - top)
                    p_new = jnp.exp(s_new - top)
                    total = jnp.sum(p_old, axis=1, keepdims=True) + jnp.sum(
                        p_new, axis=1, keepdims=True
                    )
                    part = jnp.dot(
                        p_old.astype(jnp.bfloat16), v_old, preferred_element_type=jnp.float32
                    )
                    part += jnp.dot(
                        p_new.astype(jnp.bfloat16), v_new, preferred_element_type=jnp.float32
                    )
                    part = part / total
                    mixed = jnp.zeros((TILE, span), jnp.float32)
                    for h in range(GROUP):
                        mixed = jnp.where(head_of == h, part[h * TILE : (h + 1) * TILE], mixed)
                    kept = att_ref[rows, lo : lo + span]
                    att_ref[rows, lo : lo + span] = jnp.where(
                        in_request, mixed.astype(jnp.bfloat16), kept
                    )

    out_ref[...] = jnp.dot(
        unsort_ref[...], att_ref[...], preferred_element_type=jnp.float32
    ).astype(jnp.bfloat16)


def out_kernel(back_ref, returned_ref, w_ref, tokens_ref, gain_ref, shift_ref, out_ref):
    rows = jnp.dot(
        back_ref[...], returned_ref[...], preferred_element_type=jnp.float32
    ).astype(jnp.bfloat16)
    summed = jnp.dot(rows, w_ref[...], preferred_element_type=jnp.float32)
    summed = summed + tokens_ref[...].astype(jnp.float32)
    out_ref[...] = layer_norm(summed, gain_ref[...], shift_ref[...]).astype(jnp.bfloat16)


def gelu(hidden):
    return (0.5 * hidden * (1.0 + lax.erf(hidden * (0.5**0.5)))).astype(jnp.bfloat16)


def ffn_part(x, fc1, fc2):
    hidden = gelu(jnp.dot(x, fc1, preferred_element_type=jnp.float32))
    return jnp.dot(hidden, fc2, preferred_element_type=jnp.float32)


def ffn_kernel(x_ref, fc1_ref, fc2_ref, out_ref):
    out_ref[...] = ffn_part(x_ref[...], fc1_ref[...], fc2_ref[...])


def unpack(pieces, pair_ref, width):
    pair = pair_ref[...].reshape(pieces, -1, pair_ref.shape[-1])
    rows = width // pieces
    hidden = pair.shape[1] * pieces * pair.shape[2] // width - pair.shape[2]
    return pair[:, :rows].reshape(width, -1), pair[:, rows:].reshape(hidden, width)


def own_kernel(pieces, x_ref, base_ref, pair_ref, out_ref):
    pair = unpack(pieces, pair_ref, x_ref.shape[1])
    out_ref[...] = base_ref[...] + ffn_part(x_ref[...], *pair)


def visitor_kernel(pieces, x_ref, fc1_ref, fc2_ref, pair_ref, out_ref):
    total = ffn_part(x_ref[...], fc1_ref[...], fc2_ref[...])
    pair = unpack(pieces, pair_ref, x_ref.shape[1])
    out_ref[...] = (total + ffn_part(x_ref[...], *pair)).astype(out_ref.dtype)


def final_kernel(gain_ref, shift_ref, normed_ref, *refs):
    summed = normed_ref[...].astype(jnp.float32)
    for part_ref in refs[:-1]:
        summed = summed + part_ref[...].astype(jnp.float32)
    refs[-1][...] = layer_norm(summed, gain_ref[...], shift_ref[...]).astype(jnp.bfloat16)


def piece_of(*weights):
    pieces = lax.axis_size("req")
    index = lax.axis_index("req")
    shares = [
        lax.dynamic_slice_in_dim(w, index * (w.shape[0] // pieces), w.shape[0] // pieces)
        for w in weights
    ]
    columns = min(w.shape[1] for w in weights)
    return jnp.concatenate([s.reshape(-1, columns) for s in shares], axis=0)


def vmem(n):
    return [pl.BlockSpec(memory_space=pltpu.VMEM)] * n


def hbm(n):
    return [pl.BlockSpec(memory_space=pltpu.HBM)] * n


def smem(n):
    return [pl.BlockSpec(memory_space=pltpu.SMEM)] * n


def params(limit=VMEM_LIMIT):
    return pltpu.CompilerParams(vmem_limit_bytes=limit)


def shape(dims, dtype=jnp.bfloat16):
    return jax.ShapeDtypeStruct(dims, dtype)


def per_device(
    tokens,
    token_owner,
    token_request,
    cache_len,
    cache_k,
    cache_v,
    w_qkv,
    w_out,
    w_fc1,
    w_fc2,
    ln1_gain,
    ln1_bias,
    ln2_gain,
    ln2_bias,
):
    devices = lax.axis_size(ALL)
    owner_index = lax.axis_index(ALL)
    tok_dev, width = tokens.shape
    piece = piece_of(w_fc1, w_fc2)
    capacity = max(2, 2 * tok_dev // devices)
    slots = devices * capacity
    me = owner_index.astype(jnp.int32).reshape(1)
    owners = token_owner.reshape(devices, tok_dev)
    requests = token_request.reshape(devices, tok_dev)
    outgoing = pl.pallas_call(
        functools.partial(dispatch_kernel, capacity),
        out_shape=shape((slots, width)),
        in_specs=smem(1) + vmem(2),
        out_specs=vmem(1)[0],
        compiler_params=params(16 * 1024 * 1024),
        name="dispatch",
    )(me, owners, tokens)
    arrived = lax.all_to_all(
        outgoing.reshape(devices, capacity, width),
        ALL,
        split_axis=0,
        concat_axis=0,
        tiled=True,
    )
    back, sort, unsort, starts = pl.pallas_call(
        functools.partial(table_kernel, capacity),
        out_shape=(
            shape((tok_dev, slots)),
            shape((slots, slots)),
            shape((slots, slots)),
            shape((8, 128), jnp.int32),
        ),
        in_specs=smem(1) + vmem(2),
        out_specs=tuple(vmem(4)),
        compiler_params=params(16 * 1024 * 1024),
        cost_estimate=pl.CostEstimate(flops=40_000_000, bytes_accessed=400_000, transcendentals=0),
        name="table",
    )(me, owners, requests)
    arrived, piece, back, sort, unsort, starts = lax.optimization_barrier(
        (arrived, piece, back, sort, unsort, starts)
    )
    piece = lax.ppermute(piece, "pair", [(0, 1), (1, 0)])
    attended = pl.pallas_call(
        attend_kernel,
        out_shape=shape((slots, width)),
        in_specs=smem(2) + vmem(3) + hbm(3),
        out_specs=vmem(1)[0],
        scratch_shapes=[
            pltpu.VMEM((slots, width), jnp.bfloat16),
            pltpu.VMEM((slots, 3 * width), jnp.bfloat16),
            pltpu.VMEM((slots, width), jnp.bfloat16),
            pltpu.VMEM(w_qkv.shape, jnp.bfloat16),
            pltpu.VMEM(cache_k.shape, jnp.bfloat16),
            pltpu.VMEM(cache_v.shape, jnp.bfloat16),
            pltpu.SemaphoreType.DMA((5,)),
        ],
        compiler_params=params(),
        cost_estimate=pl.CostEstimate(
            flops=16 * slots * width * width, bytes_accessed=20_000_000, transcendentals=4_000_000
        ),
        name="attend",
    )(
        starts,
        cache_len,
        sort,
        unsort,
        arrived.reshape(slots, width),
        w_qkv,
        cache_k,
        cache_v,
    )
    attended, piece = lax.optimization_barrier((attended, piece))
    pair = lax.all_gather(piece, "req", axis=0, tiled=True)
    returned = lax.all_to_all(
        attended.reshape(devices, capacity, width),
        ALL,
        split_axis=0,
        concat_axis=0,
        tiled=True,
    )
    normed = pl.pallas_call(
        out_kernel,
        out_shape=shape((tok_dev, width)),
        in_specs=vmem(6),
        out_specs=vmem(1)[0],
        compiler_params=params(16 * 1024 * 1024),
        name="out_norm",
    )(
        back,
        returned.reshape(slots, width),
        w_out,
        tokens,
        ln1_gain.reshape(1, width),
        ln1_bias.reshape(1, width),
    )
    others = lax.axis_size("other")
    pieces = lax.axis_size("req")

    def ffn_call(name, kernel, operands, dtype, pairs):
        return pl.pallas_call(
            kernel,
            out_shape=shape((tok_dev, width), dtype),
            in_specs=vmem(len(operands)),
            out_specs=vmem(1)[0],
            compiler_params=params(16 * 1024 * 1024),
            cost_estimate=pl.CostEstimate(
                flops=4 * tok_dev * w_fc1.size * pairs,
                bytes_accessed=4 * w_fc1.size * pairs,
                transcendentals=0,
            ),
            name=name,
        )(*operands)

    def shift(states, by):
        return lax.ppermute(states, "other", [(i, i ^ by) for i in range(others)])

    visitors = [shift(normed, by) for by in range(1, others)]
    own = ffn_call("ffn_own", ffn_kernel, (normed, w_fc1, w_fc2), jnp.float32, 1)
    visitors, own = lax.optimization_barrier((visitors, own))
    parts = []
    for by, visitor in enumerate(visitors, 1):
        part = ffn_call(
            "ffn_visitor",
            functools.partial(visitor_kernel, pieces),
            (visitor, w_fc1, w_fc2, pair),
            jnp.bfloat16,
            2,
        )
        parts.append(shift(part, by))
    own = ffn_call(
        "ffn_pair", functools.partial(own_kernel, pieces), (normed, own, pair), jnp.float32, 1
    )
    parts.append(own)
    return pl.pallas_call(
        final_kernel,
        out_shape=shape((tok_dev, width)),
        in_specs=vmem(len(parts) + 3),
        out_specs=vmem(1)[0],
        compiler_params=params(16 * 1024 * 1024),
        name="final_norm",
    )(ln2_gain.reshape(1, width), ln2_bias.reshape(1, width), normed, *parts)


def solution(mesh):
    n_req, n_mlp = mesh.devices.shape
    split = jax.sharding.Mesh(mesh.devices.reshape(n_req, n_mlp // 2, 2), ALL)
    mlp = ("other", "pair")
    placed = (
        P(ALL, None),
        P(),
        P(),
        P(ALL),
        P(ALL, None, None),
        P(ALL, None, None),
        P(),
        P(),
        P(None, mlp),
        P(mlp, None),
        P(),
        P(),
        P(),
        P(),
    )
    return jax.shard_map(
        per_device, mesh=split, in_specs=placed, out_specs=P(ALL, None), check_vma=False
    )
```

```python
import functools

import jax
import jax.numpy as jnp
from jax import lax
from jax.experimental import pallas as pl
from jax.experimental.pallas import tpu as pltpu
from jax.sharding import PartitionSpec as P

HEADS = 16
GROUP = 4
TILE = 80
MASKED = -1e30
VMEM_LIMIT = 56 * 1024 * 1024

ALL = ("req", "other", "pair")

epsilon = 1e-05


def layer_norm(values, gain, shift):
    center = values - jnp.mean(values, axis=-1, keepdims=True)
    spread = jnp.mean(center * center, axis=-1, keepdims=True)
    return center * lax.rsqrt(spread + epsilon) * gain + shift


def iota(shape, dim):
    return lax.broadcasted_iota(jnp.int32, shape, dim)


def own_pairs(owners_ref, me):
    tok_dev = owners_ref.shape[1]
    across = jnp.broadcast_to(owners_ref[pl.ds(me, 1), :], (tok_dev, tok_dev)).astype(jnp.float32)
    return across, across.T


def dispatch_kernel(capacity, me_ref, owners_hbm, tokens_hbm, out_ref, owners_ref, tokens_ref, sems):
    loads = [
        pltpu.make_async_copy(owners_hbm, owners_ref, sems.at[0]),
        pltpu.make_async_copy(tokens_hbm, tokens_ref, sems.at[1]),
    ]
    for load in loads:
        load.start()
    tok_dev = tokens_ref.shape[0]
    loads[0].wait()
    slots = out_ref.shape[0]
    across, down = own_pairs(owners_ref, me_ref[0])
    square = (tok_dev, tok_dev)
    earlier = (across == down) & (iota(square, 0) < iota(square, 1))
    rank = jnp.sum(jnp.where(earlier, 1.0, 0.0), axis=0, keepdims=True)
    column = across[:1, :] * capacity + rank
    onehot = iota((slots, tok_dev), 0).astype(jnp.float32) == column
    onehot = jnp.where(onehot, 1.0, 0.0).astype(jnp.bfloat16)
    loads[1].wait()
    out_ref[...] = jnp.dot(
        onehot, tokens_ref[...], preferred_element_type=jnp.float32
    ).astype(jnp.bfloat16)


def table_kernel(
    capacity, me_ref, owners_ref, requests_ref, back_ref, sort_ref, unsort_ref, starts_ref
):
    devices, tok_dev = owners_ref.shape
    slots = sort_ref.shape[0]
    me = me_ref[0]
    across, down = own_pairs(owners_ref, me)
    square = (tok_dev, tok_dev)
    earlier = (across == down) & (iota(square, 1) < iota(square, 0))
    rank = jnp.sum(jnp.where(earlier, 1.0, 0.0), axis=1, keepdims=True)
    column = down[:, :1] * capacity + rank
    back = iota((tok_dev, slots), 1).astype(jnp.float32) == column
    back_ref[...] = jnp.where(back, 1.0, 0.0).astype(jnp.bfloat16)
    mine = owners_ref[...] == me
    before = jnp.where(iota(square, 0) < iota(square, 1), 1.0, 0.0).astype(jnp.bfloat16)
    ranking = jnp.dot(
        jnp.where(mine, 1.0, 0.0).astype(jnp.bfloat16), before, preferred_element_type=jnp.float32
    ).astype(jnp.bfloat16)
    coded = jnp.where(mine, requests_ref[...] + 1, 0).astype(jnp.float32).astype(jnp.bfloat16)
    slot = iota((slots, devices), 0)
    source = iota((slots, devices), 1)
    from_here = (slot >= source * capacity) & (slot < (source + 1) * capacity)
    place = jnp.sum(jnp.where(from_here, slot - source * capacity, 0), axis=1, keepdims=True)
    from_here = jnp.where(from_here, 1.0, 0.0).astype(jnp.bfloat16)
    rank_of = jnp.dot(from_here, ranking, preferred_element_type=jnp.float32)
    code_of = jnp.dot(from_here, coded, preferred_element_type=jnp.float32)
    hit = rank_of == place.astype(jnp.float32)
    code = jnp.sum(jnp.where(hit, code_of, 0.0), axis=1, keepdims=True)
    wide = (slots, slots)
    code_i = jnp.broadcast_to(code, wide)
    code_j = code_i.T
    sub, lane = iota(wide, 0), iota(wide, 1)
    ahead_j = (code_j > 0) & ((code_j < code_i) | ((code_j == code_i) & (lane < sub)))
    ahead_i = (code_i > 0) & ((code_i < code_j) | ((code_i == code_j) & (sub < lane)))
    place_i = jnp.sum(jnp.where(ahead_j, 1.0, 0.0), axis=1, keepdims=True)
    place_j = jnp.sum(jnp.where(ahead_i, 1.0, 0.0), axis=0, keepdims=True)
    sort = (place_j == sub.astype(jnp.float32)) & (code_j > 0)
    unsort = (place_i == lane.astype(jnp.float32)) & (code_i > 0)
    sort_ref[...] = jnp.where(sort, 1.0, 0.0).astype(jnp.bfloat16)
    unsort_ref[...] = jnp.where(unsort, 1.0, 0.0).astype(jnp.bfloat16)
    few = code_j[:8, :]
    upto = (few > 0) & (few <= iota((8, slots), 0).astype(jnp.float32))
    starts = jnp.sum(jnp.where(upto, 1.0, 0.0), axis=1, keepdims=True)
    starts_ref[...] = jnp.broadcast_to(starts, starts_ref.shape).astype(jnp.int32)


def attend_kernel(
    starts_ref,
    lengths_ref,
    sort_ref,
    unsort_ref,
    x_ref,
    w_ref,
    keys_ref,
    values_ref,
    out_ref,
    sorted_ref,
    proj_ref,
    att_ref,
    w_held,
    keys_held,
    values_held,
    w_sems,
    cache_sems,
):
    slots, width = x_ref.shape
    requests, context, _ = keys_ref.shape
    head_dim = width // HEADS
    span = GROUP * head_dim
    groups = width // span
    scale = head_dim ** (-0.5)

    def w_load(part):
        columns = pl.ds(part * width, width)
        return pltpu.make_async_copy(
            w_ref.at[:, columns], w_held.at[:, columns], w_sems.at[part]
        )

    def cache_load(r, ref, held, i):
        return pltpu.make_async_copy(ref.at[r], held.at[r], cache_sems.at[r, i])

    def start_cache(r):
        cache_load(r, keys_ref, keys_held, 0).start()
        cache_load(r, values_ref, values_held, 1).start()

    ahead = min(2, requests)
    for part in range(3):
        w_load(part).start()
    sorted_ref[...] = jnp.dot(
        sort_ref[...], x_ref[...], preferred_element_type=jnp.float32
    ).astype(jnp.bfloat16)
    att_ref[...] = jnp.zeros_like(att_ref)
    for part in range(3):
        w_load(part).wait()
        if 0 < part <= ahead:
            start_cache(part - 1)

        for c in range(2):
            columns = pl.ds(part * width + c * (width // 2), width // 2)
            projected = jnp.dot(
                sorted_ref[...], w_held[:, columns], preferred_element_type=jnp.float32
            ).astype(jnp.bfloat16)
            proj_ref[:, columns] = projected

    row_step = 16
    window = min(slots, 128)
    head_of = iota((1, span), 1) // head_dim
    across = (((1,), (1,)), ((), ()))

    def attend(r, first, begin, end, length, old, new, new_first):
        rows = pl.ds(first, TILE)
        fresh = pl.ds(new_first, new)
        row = iota((TILE, 1), 0) + first
        key = iota((1, new), 1) + new_first
        new_bias = jnp.where((key >= begin) & (key <= row), 0.0, MASKED)
        new_bias = jnp.concatenate([new_bias] * GROUP, axis=0)
        old_bias = jnp.where(iota((1, old), 1) < length, 0.0, MASKED)
        mixes = []
        for g in range(groups):
            lo = g * span
            q = proj_ref[rows, lo : lo + span]
            q = jnp.concatenate(
                [jnp.where(head_of == h, q, jnp.bfloat16(0)) for h in range(GROUP)], axis=0
            )
            k_new = proj_ref[fresh, width + lo : width + lo + span]
            v_new = proj_ref[fresh, 2 * width + lo : 2 * width + lo + span]
            k_old = keys_held[r, :old, lo : lo + span]
            v_old = values_held[r, :old, lo : lo + span]
            s_old = (
                lax.dot_general(q, k_old, across, preferred_element_type=jnp.float32) * scale
                + old_bias
            )
            s_new = (
                lax.dot_general(q, k_new, across, preferred_element_type=jnp.float32) * scale
                + new_bias
            )
            top = jnp.maximum(
                jnp.max(s_old, axis=1, keepdims=True), jnp.max(s_new, axis=1, keepdims=True)
            )
            p_old = jnp.exp(s_old - top)
            p_new = jnp.exp(s_new - top)
            total = jnp.sum(p_old, axis=1, keepdims=True) + jnp.sum(p_new, axis=1, keepdims=True)
            part = jnp.dot(
                jnp.concatenate([p_old.astype(jnp.bfloat16), p_new.astype(jnp.bfloat16)], axis=1),
                jnp.concatenate([v_old, v_new], axis=0),
                preferred_element_type=jnp.float32,
            )
            part = part * (1.0 / total)
            mixed = part[:TILE]
            for h in range(1, GROUP):
                mixed = jnp.where(head_of == h, part[h * TILE : (h + 1) * TILE], mixed)
            mixes.append(mixed.astype(jnp.bfloat16))
        inside = (row >= begin) & (row < end)
        att_ref[rows, :] = jnp.where(inside, jnp.concatenate(mixes, axis=1), att_ref[rows, :])

    @pl.loop(0, requests)
    def _(r):
        cache_load(r, keys_ref, keys_held, 0).wait()
        cache_load(r, values_ref, values_held, 1).wait()

        @pl.when(r + ahead < requests)
        def _():
            start_cache(r + ahead)

        begin, end = starts_ref[r, 0], starts_ref[r + 1, 0]
        length = lengths_ref[r]
        base = begin // row_step * row_step

        @pl.loop(0, jnp.where(end > begin, pl.cdiv(end - base, TILE), 0))
        def _(t):
            first = pl.multiple_of(jnp.minimum(base + t * TILE, slots - TILE), row_step)
            new_first = pl.multiple_of(jnp.minimum(base, slots - window), row_step)
            few_new = end <= new_first + window
            few_old = length <= context // 2

            for old, is_old in ((context // 2, few_old), (context, ~few_old)):
                for new, is_new in ((window, few_new), (slots, ~few_new)):

                    @pl.when(is_old & is_new)
                    def _():
                        start = new_first if new < slots else 0
                        attend(r, first, begin, end, length, old, new, start)

    out_ref[...] = jnp.dot(
        unsort_ref[...], att_ref[...], preferred_element_type=jnp.float32
    ).astype(jnp.bfloat16)


def out_kernel(back_ref, returned_ref, w_ref, tokens_ref, gain_ref, shift_ref, out_ref):
    rows = jnp.dot(
        back_ref[...], returned_ref[...], preferred_element_type=jnp.float32
    ).astype(jnp.bfloat16)
    summed = jnp.dot(rows, w_ref[...], preferred_element_type=jnp.float32)
    summed = summed + tokens_ref[...].astype(jnp.float32)
    out_ref[...] = layer_norm(summed, gain_ref[...], shift_ref[...]).astype(jnp.bfloat16)


def gelu(hidden):
    return (0.5 * hidden * (1.0 + lax.erf(hidden * (0.5**0.5)))).astype(jnp.bfloat16)


def ffn_part(x, fc1, fc2):
    hidden = gelu(jnp.dot(x, fc1, preferred_element_type=jnp.float32))
    return jnp.dot(hidden, fc2, preferred_element_type=jnp.float32)


def ffn_kernel(x_ref, fc1_ref, fc2_ref, out_ref):
    out_ref[...] = ffn_part(x_ref[...], fc1_ref[...], fc2_ref[...])


def pair_kernel(x_ref, base_ref, pair_ref, out_ref):
    pieces = pair_ref.shape[0]
    width = x_ref.shape[1]
    rows = width // pieces
    fc1 = pair_ref[:, :rows].reshape(width, -1)
    hidden = gelu(jnp.dot(x_ref[...], fc1, preferred_element_type=jnp.float32))
    fc2 = pair_ref[:, rows:].reshape(fc1.shape[1], width)
    part = jnp.dot(hidden, fc2, preferred_element_type=jnp.float32)
    out_ref[...] = (base_ref[...] + part).astype(out_ref.dtype)


def final_kernel(gain_ref, shift_ref, normed_ref, *refs):
    summed = normed_ref[...].astype(jnp.float32)
    for part_ref in refs[:-1]:
        summed = summed + part_ref[...].astype(jnp.float32)
    refs[-1][...] = layer_norm(summed, gain_ref[...], shift_ref[...]).astype(jnp.bfloat16)


def piece_of(*weights):
    pieces = lax.axis_size("req")
    index = lax.axis_index("req")
    shares = [
        lax.dynamic_slice_in_dim(w, index * (w.shape[0] // pieces), w.shape[0] // pieces)
        for w in weights
    ]
    columns = min(w.shape[1] for w in weights)
    return jnp.concatenate([s.reshape(-1, columns) for s in shares], axis=0)


def vmem(n):
    return [pl.BlockSpec(memory_space=pltpu.VMEM)] * n


def hbm(n):
    return [pl.BlockSpec(memory_space=pltpu.HBM)] * n


def smem(n):
    return [pl.BlockSpec(memory_space=pltpu.SMEM)] * n


def params(limit=VMEM_LIMIT):
    return pltpu.CompilerParams(vmem_limit_bytes=limit)


def shape(dims, dtype=jnp.bfloat16):
    return jax.ShapeDtypeStruct(dims, dtype)


def per_device(
    tokens,
    token_owner,
    token_request,
    cache_len,
    cache_k,
    cache_v,
    w_qkv,
    w_out,
    w_fc1,
    w_fc2,
    ln1_gain,
    ln1_bias,
    ln2_gain,
    ln2_bias,
):
    devices = lax.axis_size(ALL)
    owner_index = lax.axis_index(ALL)
    tok_dev, width = tokens.shape
    piece = piece_of(w_fc1, w_fc2)
    capacity = max(2, 2 * tok_dev // devices)
    slots = devices * capacity
    me = owner_index.astype(jnp.int32).reshape(1)
    owners = token_owner.reshape(devices, tok_dev)
    requests = token_request.reshape(devices, tok_dev)
    outgoing = pl.pallas_call(
        functools.partial(dispatch_kernel, capacity),
        out_shape=shape((slots, width)),
        in_specs=smem(1) + hbm(2),
        out_specs=vmem(1)[0],
        scratch_shapes=[
            pltpu.VMEM(owners.shape, owners.dtype),
            pltpu.VMEM(tokens.shape, tokens.dtype),
            pltpu.SemaphoreType.DMA((2,)),
        ],
        compiler_params=params(),
        name="dispatch",
    )(me, owners, tokens)
    arrived = lax.all_to_all(
        outgoing.reshape(devices, capacity, width),
        ALL,
        split_axis=0,
        concat_axis=0,
        tiled=True,
    )
    back, sort, unsort, starts = pl.pallas_call(
        functools.partial(table_kernel, capacity),
        out_shape=(
            shape((tok_dev, slots)),
            shape((slots, slots)),
            shape((slots, slots)),
            shape((8, 128), jnp.int32),
        ),
        in_specs=smem(1) + vmem(2),
        out_specs=tuple(vmem(4)),
        compiler_params=params(16 * 1024 * 1024),
        cost_estimate=pl.CostEstimate(flops=40_000_000, bytes_accessed=400_000, transcendentals=0),
        name="table",
    )(me, owners, requests)
    arrived, piece, back, sort, unsort, starts = lax.optimization_barrier(
        (arrived, piece, back, sort, unsort, starts)
    )
    piece = lax.ppermute(piece, "pair", [(0, 1), (1, 0)])
    attended = pl.pallas_call(
        attend_kernel,
        out_shape=shape((slots, width)),
        in_specs=smem(2) + vmem(3) + hbm(3),
        out_specs=vmem(1)[0],
        scratch_shapes=[
            pltpu.VMEM((slots, width), jnp.bfloat16),
            pltpu.VMEM((slots, 3 * width), jnp.bfloat16),
            pltpu.VMEM((slots, width), jnp.bfloat16),
            pltpu.VMEM(w_qkv.shape, jnp.bfloat16),
            pltpu.VMEM(cache_k.shape, jnp.bfloat16),
            pltpu.VMEM(cache_v.shape, jnp.bfloat16),
            pltpu.SemaphoreType.DMA((3,)),
            pltpu.SemaphoreType.DMA((cache_k.shape[0], 2)),
        ],
        compiler_params=params(50 * 1024 * 1024),
        cost_estimate=pl.CostEstimate(
            flops=16 * slots * width * width, bytes_accessed=20_000_000, transcendentals=4_000_000
        ),
        name="attend",
    )(
        starts,
        cache_len,
        sort,
        unsort,
        arrived.reshape(slots, width),
        w_qkv,
        cache_k,
        cache_v,
    )
    attended, piece = lax.optimization_barrier((attended, piece))
    pair = lax.all_gather(piece, "req", axis=0, tiled=True)
    returned = lax.all_to_all(
        attended.reshape(devices, capacity, width),
        ALL,
        split_axis=0,
        concat_axis=0,
        tiled=True,
    )
    normed = pl.pallas_call(
        out_kernel,
        out_shape=shape((tok_dev, width)),
        in_specs=vmem(6),
        out_specs=vmem(1)[0],
        compiler_params=params(16 * 1024 * 1024),
        name="out_norm",
    )(
        back,
        returned.reshape(slots, width),
        w_out,
        tokens,
        ln1_gain.reshape(1, width),
        ln1_bias.reshape(1, width),
    )
    others = lax.axis_size("other")
    pieces = lax.axis_size("req")
    pair = pair.reshape(pieces, -1, pair.shape[1])
    cost = pl.CostEstimate(
        flops=4 * tok_dev * w_fc1.size, bytes_accessed=4 * w_fc1.size, transcendentals=0
    )

    def near_part(states):
        return pl.pallas_call(
            ffn_kernel,
            out_shape=shape((tok_dev, width), jnp.float32),
            in_specs=vmem(3),
            out_specs=vmem(1)[0],
            compiler_params=params(16 * 1024 * 1024),
            cost_estimate=cost,
            name="ffn_near",
        )(states, w_fc1, w_fc2)

    def pair_part(states, base, dtype):
        return pl.pallas_call(
            pair_kernel,
            out_shape=shape((tok_dev, width), dtype),
            in_specs=vmem(3),
            out_specs=vmem(1)[0],
            compiler_params=params(16 * 1024 * 1024),
            cost_estimate=cost,
            name="ffn_pair",
        )(states, base, pair)

    def shift(states, by):
        return lax.ppermute(states, "other", [(i, i ^ by) for i in range(others)])

    visitors = [shift(normed, by) for by in range(1, others)]
    own = near_part(normed)
    visitors, own = lax.optimization_barrier((visitors, own))
    bases = [near_part(visitor) for visitor in visitors]
    bases, pair = lax.optimization_barrier((bases, pair))
    parts = [
        shift(pair_part(visitor, base, jnp.bfloat16), by)
        for by, (visitor, base) in enumerate(zip(visitors, bases), 1)
    ]
    parts.append(pair_part(normed, own, jnp.float32))
    return pl.pallas_call(
        final_kernel,
        out_shape=shape((tok_dev, width)),
        in_specs=vmem(len(parts) + 3),
        out_specs=vmem(1)[0],
        compiler_params=params(16 * 1024 * 1024),
        name="final_norm",
    )(ln2_gain.reshape(1, width), ln2_bias.reshape(1, width), normed, *parts)


def solution(mesh):
    n_req, n_mlp = mesh.devices.shape
    split = jax.sharding.Mesh(mesh.devices.reshape(n_req, n_mlp // 2, 2), ALL)
    mlp = ("other", "pair")
    placed = (
        P(ALL, None),
        P(),
        P(),
        P(ALL),
        P(ALL, None, None),
        P(ALL, None, None),
        P(),
        P(),
        P(None, mlp),
        P(mlp, None),
        P(),
        P(),
        P(),
        P(),
    )
    return jax.shard_map(
        per_device, mesh=split, in_specs=placed, out_specs=P(ALL, None), check_vma=False
    )
```

```python
import functools

import jax
import jax.numpy as jnp
from jax import lax
from jax.experimental import pallas as pl
from jax.experimental.pallas import tpu as pltpu
from jax.sharding import PartitionSpec as P

HEADS = 16
GROUP = 4
TILE = 80
MASKED = -1e30
VMEM_LIMIT = 56 * 1024 * 1024

ALL = ("req", "other", "pair")

epsilon = 1e-05


def layer_norm(values, gain, shift):
    center = values - jnp.mean(values, axis=-1, keepdims=True)
    spread = jnp.mean(center * center, axis=-1, keepdims=True)
    return center * lax.rsqrt(spread + epsilon) * gain + shift


def iota(shape, dim):
    return lax.broadcasted_iota(jnp.int32, shape, dim)


def own_pairs(owners_ref, me):
    tok_dev = owners_ref.shape[1]
    across = jnp.broadcast_to(owners_ref[pl.ds(me, 1), :], (tok_dev, tok_dev)).astype(jnp.float32)
    return across, across.T


def dispatch_kernel(capacity, me_ref, owners_hbm, tokens_hbm, out_ref, owners_ref, tokens_ref, sems):
    loads = [
        pltpu.make_async_copy(owners_hbm, owners_ref, sems.at[0]),
        pltpu.make_async_copy(tokens_hbm, tokens_ref, sems.at[1]),
    ]
    for load in loads:
        load.start()
    tok_dev = tokens_ref.shape[0]
    loads[0].wait()
    slots = out_ref.shape[0]
    across, down = own_pairs(owners_ref, me_ref[0])
    square = (tok_dev, tok_dev)
    earlier = (across == down) & (iota(square, 0) < iota(square, 1))
    rank = jnp.sum(jnp.where(earlier, 1.0, 0.0), axis=0, keepdims=True)
    column = across[:1, :] * capacity + rank
    onehot = iota((slots, tok_dev), 0).astype(jnp.float32) == column
    onehot = jnp.where(onehot, 1.0, 0.0).astype(jnp.bfloat16)
    loads[1].wait()
    out_ref[...] = jnp.dot(
        onehot, tokens_ref[...], preferred_element_type=jnp.float32
    ).astype(jnp.bfloat16)


def table_kernel(
    capacity, me_ref, owners_ref, requests_ref, back_ref, sort_ref, unsort_ref, starts_ref
):
    devices, tok_dev = owners_ref.shape
    slots = sort_ref.shape[0]
    me = me_ref[0]
    across, down = own_pairs(owners_ref, me)
    square = (tok_dev, tok_dev)
    earlier = (across == down) & (iota(square, 1) < iota(square, 0))
    rank = jnp.sum(jnp.where(earlier, 1.0, 0.0), axis=1, keepdims=True)
    column = down[:, :1] * capacity + rank
    back = iota((tok_dev, slots), 1).astype(jnp.float32) == column
    back_ref[...] = jnp.where(back, 1.0, 0.0).astype(jnp.bfloat16)
    mine = owners_ref[...] == me
    before = jnp.where(iota(square, 0) < iota(square, 1), 1.0, 0.0).astype(jnp.bfloat16)
    ranking = jnp.dot(
        jnp.where(mine, 1.0, 0.0).astype(jnp.bfloat16), before, preferred_element_type=jnp.float32
    ).astype(jnp.bfloat16)
    coded = jnp.where(mine, requests_ref[...] + 1, 0).astype(jnp.float32).astype(jnp.bfloat16)
    slot = iota((slots, devices), 0)
    source = iota((slots, devices), 1)
    from_here = (slot >= source * capacity) & (slot < (source + 1) * capacity)
    place = jnp.sum(jnp.where(from_here, slot - source * capacity, 0), axis=1, keepdims=True)
    from_here = jnp.where(from_here, 1.0, 0.0).astype(jnp.bfloat16)
    rank_of = jnp.dot(from_here, ranking, preferred_element_type=jnp.float32)
    code_of = jnp.dot(from_here, coded, preferred_element_type=jnp.float32)
    hit = rank_of == place.astype(jnp.float32)
    code = jnp.sum(jnp.where(hit, code_of, 0.0), axis=1, keepdims=True)
    wide = (slots, slots)
    code_i = jnp.broadcast_to(code, wide)
    code_j = code_i.T
    sub, lane = iota(wide, 0), iota(wide, 1)
    ahead_j = (code_j > 0) & ((code_j < code_i) | ((code_j == code_i) & (lane < sub)))
    ahead_i = (code_i > 0) & ((code_i < code_j) | ((code_i == code_j) & (sub < lane)))
    place_i = jnp.sum(jnp.where(ahead_j, 1.0, 0.0), axis=1, keepdims=True)
    place_j = jnp.sum(jnp.where(ahead_i, 1.0, 0.0), axis=0, keepdims=True)
    sort = (place_j == sub.astype(jnp.float32)) & (code_j > 0)
    unsort = (place_i == lane.astype(jnp.float32)) & (code_i > 0)
    sort_ref[...] = jnp.where(sort, 1.0, 0.0).astype(jnp.bfloat16)
    unsort_ref[...] = jnp.where(unsort, 1.0, 0.0).astype(jnp.bfloat16)
    few = code_j[:8, :]
    upto = (few > 0) & (few <= iota((8, slots), 0).astype(jnp.float32))
    starts = jnp.sum(jnp.where(upto, 1.0, 0.0), axis=1, keepdims=True)
    starts_ref[...] = jnp.broadcast_to(starts, starts_ref.shape).astype(jnp.int32)


def attend_kernel(
    starts_ref,
    lengths_ref,
    sort_ref,
    unsort_ref,
    x_ref,
    w_ref,
    keys_ref,
    values_ref,
    out_ref,
    sorted_ref,
    proj_ref,
    att_ref,
    w_held,
    keys_held,
    values_held,
    w_sems,
    cache_sems,
):
    slots, width = x_ref.shape
    requests, context, _ = keys_ref.shape
    head_dim = width // HEADS
    span = GROUP * head_dim
    groups = width // span
    scale = head_dim ** (-0.5)

    def w_load(part):
        columns = pl.ds(part * width, width)
        return pltpu.make_async_copy(
            w_ref.at[:, columns], w_held.at[:, columns], w_sems.at[part]
        )

    def cache_load(r, ref, held, i):
        return pltpu.make_async_copy(ref.at[r], held.at[r], cache_sems.at[r, i])

    def start_cache(r):
        cache_load(r, keys_ref, keys_held, 0).start()
        cache_load(r, values_ref, values_held, 1).start()

    ahead = min(2, requests)
    for part in range(3):
        w_load(part).start()
    sorted_ref[...] = jnp.dot(
        sort_ref[...], x_ref[...], preferred_element_type=jnp.float32
    ).astype(jnp.bfloat16)
    att_ref[...] = jnp.zeros_like(att_ref)
    for part in range(3):
        w_load(part).wait()
        if 0 < part <= ahead:
            start_cache(part - 1)

        for c in range(2):
            columns = pl.ds(part * width + c * (width // 2), width // 2)
            projected = jnp.dot(
                sorted_ref[...], w_held[:, columns], preferred_element_type=jnp.float32
            ).astype(jnp.bfloat16)
            proj_ref[:, columns] = projected

    row_step = 16
    window = min(slots, 128)
    head_of = iota((1, span), 1) // head_dim
    across = (((1,), (1,)), ((), ()))

    def attend(r, first, begin, end, length, old, new, new_first):
        rows = pl.ds(first, TILE)
        fresh = pl.ds(new_first, new)
        row = iota((TILE, 1), 0) + first
        key = iota((1, new), 1) + new_first
        new_bias = jnp.where((key >= begin) & (key <= row), 0.0, MASKED)
        new_bias = jnp.concatenate([new_bias] * GROUP, axis=0)
        old_bias = jnp.where(iota((1, old), 1) < length, 0.0, MASKED)
        mixes = []
        for g in range(groups):
            lo = g * span
            q = proj_ref[rows, lo : lo + span]
            q = jnp.concatenate(
                [jnp.where(head_of == h, q, jnp.bfloat16(0)) for h in range(GROUP)], axis=0
            )
            k_new = proj_ref[fresh, width + lo : width + lo + span]
            v_new = proj_ref[fresh, 2 * width + lo : 2 * width + lo + span]
            k_old = keys_held[r, :old, lo : lo + span]
            v_old = values_held[r, :old, lo : lo + span]
            s_old = (
                lax.dot_general(q, k_old, across, preferred_element_type=jnp.float32) * scale
                + old_bias
            )
            s_new = (
                lax.dot_general(q, k_new, across, preferred_element_type=jnp.float32) * scale
                + new_bias
            )
            top = jnp.maximum(
                jnp.max(s_old, axis=1, keepdims=True), jnp.max(s_new, axis=1, keepdims=True)
            )
            p_old = jnp.exp(s_old - top)
            p_new = jnp.exp(s_new - top)
            total = jnp.sum(p_old, axis=1, keepdims=True) + jnp.sum(p_new, axis=1, keepdims=True)
            part = jnp.dot(
                jnp.concatenate([p_old.astype(jnp.bfloat16), p_new.astype(jnp.bfloat16)], axis=1),
                jnp.concatenate([v_old, v_new], axis=0),
                preferred_element_type=jnp.float32,
            )
            part = part * (1.0 / total)
            mixed = part[:TILE]
            for h in range(1, GROUP):
                mixed = jnp.where(head_of == h, part[h * TILE : (h + 1) * TILE], mixed)
            mixes.append(mixed.astype(jnp.bfloat16))
        inside = (row >= begin) & (row < end)
        att_ref[rows, :] = jnp.where(inside, jnp.concatenate(mixes, axis=1), att_ref[rows, :])

    @pl.loop(0, requests)
    def _(r):
        cache_load(r, keys_ref, keys_held, 0).wait()
        cache_load(r, values_ref, values_held, 1).wait()

        @pl.when(r + ahead < requests)
        def _():
            start_cache(r + ahead)

        begin, end = starts_ref[r, 0], starts_ref[r + 1, 0]
        length = lengths_ref[r]
        base = begin // row_step * row_step

        @pl.loop(0, jnp.where(end > begin, pl.cdiv(end - base, TILE), 0))
        def _(t):
            first = pl.multiple_of(jnp.minimum(base + t * TILE, slots - TILE), row_step)
            new_first = pl.multiple_of(jnp.minimum(base, slots - window), row_step)
            few_new = end <= new_first + window
            few_old = length <= context // 2

            for old, is_old in ((context // 2, few_old), (context, ~few_old)):
                for new, is_new in ((window, few_new), (slots, ~few_new)):

                    @pl.when(is_old & is_new)
                    def _():
                        start = new_first if new < slots else 0
                        attend(r, first, begin, end, length, old, new, start)

    out_ref[...] = jnp.dot(
        unsort_ref[...], att_ref[...], preferred_element_type=jnp.float32
    ).astype(jnp.bfloat16)


def out_kernel(back_ref, returned_ref, w_ref, tokens_ref, gain_ref, shift_ref, out_ref):
    rows = jnp.dot(
        back_ref[...], returned_ref[...], preferred_element_type=jnp.float32
    ).astype(jnp.bfloat16)
    summed = jnp.dot(rows, w_ref[...], preferred_element_type=jnp.float32)
    summed = summed + tokens_ref[...].astype(jnp.float32)
    out_ref[...] = layer_norm(summed, gain_ref[...], shift_ref[...]).astype(jnp.bfloat16)


def gelu(hidden):
    return (0.5 * hidden * (1.0 + lax.erf(hidden * (0.5**0.5)))).astype(jnp.bfloat16)


def ffn_part(x, fc1, fc2):
    hidden = gelu(jnp.dot(x, fc1, preferred_element_type=jnp.float32))
    return jnp.dot(hidden, fc2, preferred_element_type=jnp.float32)


def ffn_kernel(x_ref, fc1_ref, fc2_ref, out_ref):
    out_ref[...] = ffn_part(x_ref[...], fc1_ref[...], fc2_ref[...])


def pair_kernel(x_ref, base_ref, pair_ref, out_ref):
    pieces = pair_ref.shape[0]
    width = x_ref.shape[1]
    rows = width // pieces
    fc1 = pair_ref[:, :rows].reshape(width, -1)
    hidden = gelu(jnp.dot(x_ref[...], fc1, preferred_element_type=jnp.float32))
    fc2 = pair_ref[:, rows:].reshape(fc1.shape[1], width)
    part = jnp.dot(hidden, fc2, preferred_element_type=jnp.float32)
    out_ref[...] = (base_ref[...] + part).astype(out_ref.dtype)


def assemble_kernel(me_ref, *refs):
    pieces, (fc1_ref, fc2_ref, sems) = refs[:-3], refs[-3:]
    rows = fc1_ref.shape[0] // len(pieces)
    copies = []
    for k, piece in enumerate(pieces):
        place = pl.ds(pl.multiple_of((me_ref[0] ^ k) * rows, rows), rows)
        for i, out_ref in enumerate((fc1_ref, fc2_ref)):
            copies.append(
                pltpu.make_async_copy(
                    piece.at[i * rows : (i + 1) * rows], out_ref.at[place], sems.at[i, k]
                )
            )
    for copy in copies:
        copy.start()
    for copy in copies:
        copy.wait()


def whole_kernel(x_ref, fc1_ref, fc2_ref, pair_fc1_ref, pair_fc2_ref, out_ref):
    total = ffn_part(x_ref[...], fc1_ref[...], fc2_ref[...])
    total += ffn_part(x_ref[...], pair_fc1_ref[...], pair_fc2_ref[...])
    out_ref[...] = total.astype(out_ref.dtype)


def final_kernel(halves, gain_ref, shift_ref, normed_ref, own_ref, *refs):
    summed = normed_ref[...].astype(jnp.float32) + own_ref[...]
    for i in range(0, len(refs) - 1, halves):
        part = jnp.concatenate([ref[...] for ref in refs[i : i + halves]], axis=0)
        summed = summed + part.astype(jnp.float32)
    refs[-1][...] = layer_norm(summed, gain_ref[...], shift_ref[...]).astype(jnp.bfloat16)


def piece_of(*weights):
    pieces = lax.axis_size("req")
    index = lax.axis_index("req")
    shares = [
        lax.dynamic_slice_in_dim(w, index * (w.shape[0] // pieces), w.shape[0] // pieces)
        for w in weights
    ]
    columns = min(w.shape[1] for w in weights)
    return jnp.concatenate([s.reshape(-1, columns) for s in shares], axis=0)


def vmem(n):
    return [pl.BlockSpec(memory_space=pltpu.VMEM)] * n


def hbm(n):
    return [pl.BlockSpec(memory_space=pltpu.HBM)] * n


def smem(n):
    return [pl.BlockSpec(memory_space=pltpu.SMEM)] * n


def params(limit=VMEM_LIMIT):
    return pltpu.CompilerParams(vmem_limit_bytes=limit)


def shape(dims, dtype=jnp.bfloat16):
    return jax.ShapeDtypeStruct(dims, dtype)


def per_device(
    tokens,
    token_owner,
    token_request,
    cache_len,
    cache_k,
    cache_v,
    w_qkv,
    w_out,
    w_fc1,
    w_fc2,
    ln1_gain,
    ln1_bias,
    ln2_gain,
    ln2_bias,
):
    devices = lax.axis_size(ALL)
    owner_index = lax.axis_index(ALL)
    tok_dev, width = tokens.shape
    piece = piece_of(w_fc1, w_fc2)
    capacity = max(2, 2 * tok_dev // devices)
    slots = devices * capacity
    me = owner_index.astype(jnp.int32).reshape(1)
    owners = token_owner.reshape(devices, tok_dev)
    requests = token_request.reshape(devices, tok_dev)
    outgoing = pl.pallas_call(
        functools.partial(dispatch_kernel, capacity),
        out_shape=shape((slots, width)),
        in_specs=smem(1) + hbm(2),
        out_specs=vmem(1)[0],
        scratch_shapes=[
            pltpu.VMEM(owners.shape, owners.dtype),
            pltpu.VMEM(tokens.shape, tokens.dtype),
            pltpu.SemaphoreType.DMA((2,)),
        ],
        compiler_params=params(),
        name="dispatch",
    )(me, owners, tokens)
    arrived = lax.all_to_all(
        outgoing.reshape(devices, capacity, width),
        ALL,
        split_axis=0,
        concat_axis=0,
        tiled=True,
    )
    back, sort, unsort, starts = pl.pallas_call(
        functools.partial(table_kernel, capacity),
        out_shape=(
            shape((tok_dev, slots)),
            shape((slots, slots)),
            shape((slots, slots)),
            shape((8, 128), jnp.int32),
        ),
        in_specs=smem(1) + vmem(2),
        out_specs=tuple(vmem(4)),
        compiler_params=params(16 * 1024 * 1024),
        cost_estimate=pl.CostEstimate(flops=40_000_000, bytes_accessed=400_000, transcendentals=0),
        name="table",
    )(me, owners, requests)
    arrived, piece, back, sort, unsort, starts = lax.optimization_barrier(
        (arrived, piece, back, sort, unsort, starts)
    )
    piece = lax.ppermute(piece, "pair", [(0, 1), (1, 0)])
    attended = pl.pallas_call(
        attend_kernel,
        out_shape=shape((slots, width)),
        in_specs=smem(2) + vmem(3) + hbm(3),
        out_specs=vmem(1)[0],
        scratch_shapes=[
            pltpu.VMEM((slots, width), jnp.bfloat16),
            pltpu.VMEM((slots, 3 * width), jnp.bfloat16),
            pltpu.VMEM((slots, width), jnp.bfloat16),
            pltpu.VMEM(w_qkv.shape, jnp.bfloat16),
            pltpu.VMEM(cache_k.shape, jnp.bfloat16),
            pltpu.VMEM(cache_v.shape, jnp.bfloat16),
            pltpu.SemaphoreType.DMA((3,)),
            pltpu.SemaphoreType.DMA((cache_k.shape[0], 2)),
        ],
        compiler_params=params(50 * 1024 * 1024),
        cost_estimate=pl.CostEstimate(
            flops=16 * slots * width * width, bytes_accessed=20_000_000, transcendentals=4_000_000
        ),
        name="attend",
    )(
        starts,
        cache_len,
        sort,
        unsort,
        arrived.reshape(slots, width),
        w_qkv,
        cache_k,
        cache_v,
    )
    attended, piece = lax.optimization_barrier((attended, piece))
    sharers = lax.axis_size("req")
    rows = w_fc1.shape[0] // sharers
    by_permutes = rows % 128 == 0 and w_fc1.shape[0] == w_fc1.shape[1]

    def from_sharer(piece, by):
        return lax.ppermute(piece, "req", [(i, i ^ by) for i in range(sharers)])

    if by_permutes:
        mate = from_sharer(piece, 1)
        shares = [from_sharer(piece, by) for by in range(2, sharers, 2)]
    else:
        pair = lax.all_gather(piece, "req", axis=0, tiled=True)
    returned = lax.all_to_all(
        attended.reshape(devices, capacity, width),
        ALL,
        split_axis=0,
        concat_axis=0,
        tiled=True,
    )
    normed = pl.pallas_call(
        out_kernel,
        out_shape=shape((tok_dev, width)),
        in_specs=vmem(6),
        out_specs=vmem(1)[0],
        compiler_params=params(16 * 1024 * 1024),
        name="out_norm",
    )(
        back,
        returned.reshape(slots, width),
        w_out,
        tokens,
        ln1_gain.reshape(1, width),
        ln1_bias.reshape(1, width),
    )
    others = lax.axis_size("other")
    cost = pl.CostEstimate(
        flops=4 * tok_dev * w_fc1.size, bytes_accessed=4 * w_fc1.size, transcendentals=0
    )

    def near_part(states):
        return pl.pallas_call(
            ffn_kernel,
            out_shape=shape((tok_dev, width), jnp.float32),
            in_specs=vmem(3),
            out_specs=vmem(1)[0],
            compiler_params=params(16 * 1024 * 1024),
            cost_estimate=cost,
            name="ffn_near",
        )(states, w_fc1, w_fc2)

    def pair_part(states, base, dtype):
        return pl.pallas_call(
            pair_kernel,
            out_shape=shape((tok_dev, width), dtype),
            in_specs=vmem(3),
            out_specs=vmem(1)[0],
            compiler_params=params(16 * 1024 * 1024),
            cost_estimate=cost,
            name="ffn_pair",
        )(states, base, pair)

    def shift(states, by):
        return lax.ppermute(states, "other", [(i, i ^ by) for i in range(others)])

    if by_permutes:
        halves = 2
        half = tok_dev // halves
        visitors = [
            [shift(normed[i * half : (i + 1) * half], by) for i in range(halves)]
            for by in range(1, others)
        ]
        shares, visitors[0][0] = lax.optimization_barrier((shares, visitors[0][0]))
        shares = [piece, mate] + [got for s in shares for got in (s, from_sharer(s, 1))]
        me_req = lax.axis_index("req").astype(jnp.int32).reshape(1)
        pair_weights = pl.pallas_call(
            assemble_kernel,
            out_shape=(shape(w_fc1.shape), shape(w_fc2.shape)),
            in_specs=smem(1) + vmem(len(shares)),
            out_specs=tuple(vmem(2)),
            scratch_shapes=[pltpu.SemaphoreType.DMA((2, len(shares)))],
            compiler_params=params(16 * 1024 * 1024),
            cost_estimate=cost,
            name="assemble",
        )(me_req, *shares)

        def whole(states, dtype):
            return pl.pallas_call(
                whole_kernel,
                out_shape=shape(states.shape, dtype),
                in_specs=vmem(5),
                out_specs=vmem(1)[0],
                compiler_params=params(16 * 1024 * 1024),
                cost_estimate=cost,
                name="ffn_whole",
            )(states, w_fc1, w_fc2, *pair_weights)

        parts = []
        for by, pair_visitors in enumerate(visitors, 1):
            parts += [shift(whole(visitor, jnp.bfloat16), by) for visitor in pair_visitors]
        own = whole(normed, jnp.float32)
    else:
        halves = 1
        pair = pair.reshape(sharers, -1, pair.shape[1])
        visitors = [shift(normed, by) for by in range(1, others)]
        own = near_part(normed)
        visitors, own = lax.optimization_barrier((visitors, own))
        bases = [near_part(visitor) for visitor in visitors]
        bases, pair = lax.optimization_barrier((bases, pair))
        parts = [
            shift(pair_part(visitor, base, jnp.bfloat16), by)
            for by, (visitor, base) in enumerate(zip(visitors, bases), 1)
        ]
        own = pair_part(normed, own, jnp.float32)
    return pl.pallas_call(
        functools.partial(final_kernel, halves),
        out_shape=shape((tok_dev, width)),
        in_specs=vmem(len(parts) + 4),
        out_specs=vmem(1)[0],
        compiler_params=params(16 * 1024 * 1024),
        name="final_norm",
    )(ln2_gain.reshape(1, width), ln2_bias.reshape(1, width), normed, own, *parts)


def solution(mesh):
    n_req, n_mlp = mesh.devices.shape
    split = jax.sharding.Mesh(mesh.devices.reshape(n_req, n_mlp // 2, 2), ALL)
    mlp = ("other", "pair")
    placed = (
        P(ALL, None),
        P(),
        P(),
        P(ALL),
        P(ALL, None, None),
        P(ALL, None, None),
        P(),
        P(),
        P(None, mlp),
        P(mlp, None),
        P(),
        P(),
        P(),
        P(),
    )
    return jax.shard_map(
        per_device, mesh=split, in_specs=placed, out_specs=P(ALL, None), check_vma=False
    )
```

```python
import functools

import jax
import jax.numpy as jnp
from jax import lax
from jax.experimental import pallas as pl
from jax.experimental.pallas import tpu as pltpu
from jax.sharding import PartitionSpec as P

HEADS = 16
GROUP = 4
TILE = 80
MASKED = -1e30
VMEM_LIMIT = 56 * 1024 * 1024

ALL = ("req", "other", "pair")

epsilon = 1e-05


def layer_norm(values, gain, shift):
    center = values - jnp.mean(values, axis=-1, keepdims=True)
    spread = jnp.mean(center * center, axis=-1, keepdims=True)
    return center * lax.rsqrt(spread + epsilon) * gain + shift


def iota(shape, dim):
    return lax.broadcasted_iota(jnp.int32, shape, dim)


def own_pairs(owners_ref, me):
    tok_dev = owners_ref.shape[1]
    across = jnp.broadcast_to(owners_ref[pl.ds(me, 1), :], (tok_dev, tok_dev)).astype(jnp.float32)
    return across, across.T


def dispatch_kernel(capacity, me_ref, owners_hbm, tokens_hbm, out_ref, owners_ref, tokens_ref, sems):
    loads = [
        pltpu.make_async_copy(owners_hbm, owners_ref, sems.at[0]),
        pltpu.make_async_copy(tokens_hbm, tokens_ref, sems.at[1]),
    ]
    for load in loads:
        load.start()
    tok_dev = tokens_ref.shape[0]
    loads[0].wait()
    slots = out_ref.shape[0]
    across, down = own_pairs(owners_ref, me_ref[0])
    square = (tok_dev, tok_dev)
    earlier = (across == down) & (iota(square, 0) < iota(square, 1))
    rank = jnp.sum(jnp.where(earlier, 1.0, 0.0), axis=0, keepdims=True)
    column = across[:1, :] * capacity + rank
    onehot = iota((slots, tok_dev), 0).astype(jnp.float32) == column
    onehot = jnp.where(onehot, 1.0, 0.0).astype(jnp.bfloat16)
    loads[1].wait()
    out_ref[...] = jnp.dot(
        onehot, tokens_ref[...], preferred_element_type=jnp.float32
    ).astype(jnp.bfloat16)


def table_kernel(
    capacity, me_ref, owners_ref, requests_ref, back_ref, sort_ref, unsort_ref, starts_ref
):
    devices, tok_dev = owners_ref.shape
    slots = sort_ref.shape[0]
    me = me_ref[0]
    across, down = own_pairs(owners_ref, me)
    square = (tok_dev, tok_dev)
    earlier = (across == down) & (iota(square, 1) < iota(square, 0))
    rank = jnp.sum(jnp.where(earlier, 1.0, 0.0), axis=1, keepdims=True)
    column = down[:, :1] * capacity + rank
    back = iota((tok_dev, slots), 1).astype(jnp.float32) == column
    back_ref[...] = jnp.where(back, 1.0, 0.0).astype(jnp.bfloat16)
    mine = owners_ref[...] == me
    before = jnp.where(iota(square, 0) < iota(square, 1), 1.0, 0.0).astype(jnp.bfloat16)
    ranking = jnp.dot(
        jnp.where(mine, 1.0, 0.0).astype(jnp.bfloat16), before, preferred_element_type=jnp.float32
    ).astype(jnp.bfloat16)
    coded = jnp.where(mine, requests_ref[...] + 1, 0).astype(jnp.float32).astype(jnp.bfloat16)
    slot = iota((slots, devices), 0)
    source = iota((slots, devices), 1)
    from_here = (slot >= source * capacity) & (slot < (source + 1) * capacity)
    place = jnp.sum(jnp.where(from_here, slot - source * capacity, 0), axis=1, keepdims=True)
    from_here = jnp.where(from_here, 1.0, 0.0).astype(jnp.bfloat16)
    rank_of = jnp.dot(from_here, ranking, preferred_element_type=jnp.float32)
    code_of = jnp.dot(from_here, coded, preferred_element_type=jnp.float32)
    hit = rank_of == place.astype(jnp.float32)
    code = jnp.sum(jnp.where(hit, code_of, 0.0), axis=1, keepdims=True)
    wide = (slots, slots)
    code_i = jnp.broadcast_to(code, wide)
    code_j = code_i.T
    sub, lane = iota(wide, 0), iota(wide, 1)
    ahead_j = (code_j > 0) & ((code_j < code_i) | ((code_j == code_i) & (lane < sub)))
    ahead_i = (code_i > 0) & ((code_i < code_j) | ((code_i == code_j) & (sub < lane)))
    place_i = jnp.sum(jnp.where(ahead_j, 1.0, 0.0), axis=1, keepdims=True)
    place_j = jnp.sum(jnp.where(ahead_i, 1.0, 0.0), axis=0, keepdims=True)
    sort = (place_j == sub.astype(jnp.float32)) & (code_j > 0)
    unsort = (place_i == lane.astype(jnp.float32)) & (code_i > 0)
    sort_ref[...] = jnp.where(sort, 1.0, 0.0).astype(jnp.bfloat16)
    unsort_ref[...] = jnp.where(unsort, 1.0, 0.0).astype(jnp.bfloat16)
    few = code_j[:8, :]
    upto = (few > 0) & (few <= iota((8, slots), 0).astype(jnp.float32))
    starts = jnp.sum(jnp.where(upto, 1.0, 0.0), axis=1, keepdims=True)
    starts_ref[...] = jnp.broadcast_to(starts, starts_ref.shape).astype(jnp.int32)


def attend_kernel(
    starts_ref,
    lengths_ref,
    sort_ref,
    unsort_ref,
    x_ref,
    w_ref,
    keys_ref,
    values_ref,
    out_ref,
    sorted_ref,
    proj_ref,
    att_ref,
    w_held,
    keys_held,
    values_held,
    w_sems,
    cache_sems,
):
    slots, width = x_ref.shape
    requests, context, _ = keys_ref.shape
    head_dim = width // HEADS
    span = GROUP * head_dim
    groups = width // span
    scale = head_dim ** (-0.5)

    def w_load(part):
        columns = pl.ds(part * width, width)
        return pltpu.make_async_copy(
            w_ref.at[:, columns], w_held.at[:, columns], w_sems.at[part]
        )

    def cache_load(r, ref, held, i):
        return pltpu.make_async_copy(ref.at[r], held.at[r], cache_sems.at[r, i])

    def start_cache(r):
        cache_load(r, keys_ref, keys_held, 0).start()
        cache_load(r, values_ref, values_held, 1).start()

    ahead = min(2, requests)
    for part in range(3):
        w_load(part).start()
    sorted_ref[...] = jnp.dot(
        sort_ref[...], x_ref[...], preferred_element_type=jnp.float32
    ).astype(jnp.bfloat16)
    att_ref[...] = jnp.zeros_like(att_ref)
    for part in range(3):
        w_load(part).wait()
        if 0 < part <= ahead:
            start_cache(part - 1)

        for c in range(2):
            columns = pl.ds(part * width + c * (width // 2), width // 2)
            projected = jnp.dot(
                sorted_ref[...], w_held[:, columns], preferred_element_type=jnp.float32
            ).astype(jnp.bfloat16)
            proj_ref[:, columns] = projected

    row_step = 16
    window = min(slots, 128)
    head_of = iota((1, span), 1) // head_dim
    across = (((1,), (1,)), ((), ()))

    def attend(r, first, begin, end, length, old, new, new_first):
        rows = pl.ds(first, TILE)
        fresh = pl.ds(new_first, new)
        row = iota((TILE, 1), 0) + first
        key = iota((1, new), 1) + new_first
        new_bias = jnp.where((key >= begin) & (key <= row), 0.0, MASKED)
        new_bias = jnp.concatenate([new_bias] * GROUP, axis=0)
        old_bias = jnp.where(iota((1, old), 1) < length, 0.0, MASKED)
        mixes = []
        for g in range(groups):
            lo = g * span
            q = proj_ref[rows, lo : lo + span]
            q = jnp.concatenate(
                [jnp.where(head_of == h, q, jnp.bfloat16(0)) for h in range(GROUP)], axis=0
            )
            k_new = proj_ref[fresh, width + lo : width + lo + span]
            v_new = proj_ref[fresh, 2 * width + lo : 2 * width + lo + span]
            k_old = keys_held[r, :old, lo : lo + span]
            v_old = values_held[r, :old, lo : lo + span]
            s_old = (
                lax.dot_general(q, k_old, across, preferred_element_type=jnp.float32) * scale
                + old_bias
            )
            s_new = (
                lax.dot_general(q, k_new, across, preferred_element_type=jnp.float32) * scale
                + new_bias
            )
            top = jnp.maximum(
                jnp.max(s_old, axis=1, keepdims=True), jnp.max(s_new, axis=1, keepdims=True)
            )
            p_old = jnp.exp(s_old - top)
            p_new = jnp.exp(s_new - top)
            total = jnp.sum(p_old, axis=1, keepdims=True) + jnp.sum(p_new, axis=1, keepdims=True)
            part = jnp.dot(
                jnp.concatenate([p_old.astype(jnp.bfloat16), p_new.astype(jnp.bfloat16)], axis=1),
                jnp.concatenate([v_old, v_new], axis=0),
                preferred_element_type=jnp.float32,
            )
            part = part * (1.0 / total)
            mixed = part[:TILE]
            for h in range(1, GROUP):
                mixed = jnp.where(head_of == h, part[h * TILE : (h + 1) * TILE], mixed)
            mixes.append(mixed.astype(jnp.bfloat16))
        inside = (row >= begin) & (row < end)
        att_ref[rows, :] = jnp.where(inside, jnp.concatenate(mixes, axis=1), att_ref[rows, :])

    @pl.loop(0, requests)
    def _(r):
        cache_load(r, keys_ref, keys_held, 0).wait()
        cache_load(r, values_ref, values_held, 1).wait()

        @pl.when(r + ahead < requests)
        def _():
            start_cache(r + ahead)

        begin, end = starts_ref[r, 0], starts_ref[r + 1, 0]
        length = lengths_ref[r]
        base = begin // row_step * row_step

        @pl.loop(0, jnp.where(end > begin, pl.cdiv(end - base, TILE), 0))
        def _(t):
            first = pl.multiple_of(jnp.minimum(base + t * TILE, slots - TILE), row_step)
            new_first = pl.multiple_of(jnp.minimum(base, slots - window), row_step)
            few_new = end <= new_first + window
            few_old = length <= context // 2

            for old, is_old in ((context // 2, few_old), (context, ~few_old)):
                for new, is_new in ((window, few_new), (slots, ~few_new)):

                    @pl.when(is_old & is_new)
                    def _():
                        start = new_first if new < slots else 0
                        attend(r, first, begin, end, length, old, new, start)

    out_ref[...] = jnp.dot(
        unsort_ref[...], att_ref[...], preferred_element_type=jnp.float32
    ).astype(jnp.bfloat16)


def out_kernel(back_ref, returned_ref, w_ref, tokens_ref, gain_ref, shift_ref, out_ref):
    rows = jnp.dot(
        back_ref[...], returned_ref[...], preferred_element_type=jnp.float32
    ).astype(jnp.bfloat16)
    summed = jnp.dot(rows, w_ref[...], preferred_element_type=jnp.float32)
    summed = summed + tokens_ref[...].astype(jnp.float32)
    out_ref[...] = layer_norm(summed, gain_ref[...], shift_ref[...]).astype(jnp.bfloat16)


def gelu(hidden):
    return (0.5 * hidden * (1.0 + lax.erf(hidden * (0.5**0.5)))).astype(jnp.bfloat16)


def ffn_part(x, fc1, fc2):
    hidden = gelu(jnp.dot(x, fc1, preferred_element_type=jnp.float32))
    return jnp.dot(hidden, fc2, preferred_element_type=jnp.float32)


def ffn_kernel(x_ref, fc1_ref, fc2_ref, out_ref):
    out_ref[...] = ffn_part(x_ref[...], fc1_ref[...], fc2_ref[...])


def pair_kernel(x_ref, base_ref, pair_ref, out_ref):
    pieces = pair_ref.shape[0]
    width = x_ref.shape[1]
    rows = width // pieces
    fc1 = pair_ref[:, :rows].reshape(width, -1)
    hidden = gelu(jnp.dot(x_ref[...], fc1, preferred_element_type=jnp.float32))
    fc2 = pair_ref[:, rows:].reshape(fc1.shape[1], width)
    part = jnp.dot(hidden, fc2, preferred_element_type=jnp.float32)
    out_ref[...] = (base_ref[...] + part).astype(out_ref.dtype)


def assemble_kernel(me_ref, *refs):
    pieces, (fc1_ref, fc2_ref, sems) = refs[:-3], refs[-3:]
    rows = fc1_ref.shape[0] // len(pieces)
    copies = []
    for k, piece in enumerate(pieces):
        place = pl.ds(pl.multiple_of((me_ref[0] ^ k) * rows, rows), rows)
        for i, out_ref in enumerate((fc1_ref, fc2_ref)):
            copies.append(
                pltpu.make_async_copy(
                    piece.at[i * rows : (i + 1) * rows], out_ref.at[place], sems.at[i, k]
                )
            )
    for copy in copies:
        copy.start()
    for copy in copies:
        copy.wait()


def add_kernel(x_ref, base_ref, fc1_ref, fc2_ref, out_ref):
    total = base_ref[...] + ffn_part(x_ref[...], fc1_ref[...], fc2_ref[...])
    out_ref[...] = total.astype(out_ref.dtype)


def final_kernel(halves, gain_ref, shift_ref, normed_ref, own_ref, *refs):
    summed = normed_ref[...].astype(jnp.float32) + own_ref[...]
    for i in range(0, len(refs) - 1, halves):
        part = jnp.concatenate([ref[...] for ref in refs[i : i + halves]], axis=0)
        summed = summed + part.astype(jnp.float32)
    refs[-1][...] = layer_norm(summed, gain_ref[...], shift_ref[...]).astype(jnp.bfloat16)


def piece_of(*weights):
    pieces = lax.axis_size("req")
    index = lax.axis_index("req")
    shares = [
        lax.dynamic_slice_in_dim(w, index * (w.shape[0] // pieces), w.shape[0] // pieces)
        for w in weights
    ]
    columns = min(w.shape[1] for w in weights)
    return jnp.concatenate([s.reshape(-1, columns) for s in shares], axis=0)


def vmem(n):
    return [pl.BlockSpec(memory_space=pltpu.VMEM)] * n


def hbm(n):
    return [pl.BlockSpec(memory_space=pltpu.HBM)] * n


def smem(n):
    return [pl.BlockSpec(memory_space=pltpu.SMEM)] * n


def params(limit=VMEM_LIMIT):
    return pltpu.CompilerParams(vmem_limit_bytes=limit)


def shape(dims, dtype=jnp.bfloat16):
    return jax.ShapeDtypeStruct(dims, dtype)


def per_device(
    tokens,
    token_owner,
    token_request,
    cache_len,
    cache_k,
    cache_v,
    w_qkv,
    w_out,
    w_fc1,
    w_fc2,
    ln1_gain,
    ln1_bias,
    ln2_gain,
    ln2_bias,
):
    devices = lax.axis_size(ALL)
    owner_index = lax.axis_index(ALL)
    tok_dev, width = tokens.shape
    piece = piece_of(w_fc1, w_fc2)
    capacity = max(2, 2 * tok_dev // devices)
    slots = devices * capacity
    me = owner_index.astype(jnp.int32).reshape(1)
    owners = token_owner.reshape(devices, tok_dev)
    requests = token_request.reshape(devices, tok_dev)
    outgoing = pl.pallas_call(
        functools.partial(dispatch_kernel, capacity),
        out_shape=shape((slots, width)),
        in_specs=smem(1) + hbm(2),
        out_specs=vmem(1)[0],
        scratch_shapes=[
            pltpu.VMEM(owners.shape, owners.dtype),
            pltpu.VMEM(tokens.shape, tokens.dtype),
            pltpu.SemaphoreType.DMA((2,)),
        ],
        compiler_params=params(),
        name="dispatch",
    )(me, owners, tokens)
    arrived = lax.all_to_all(
        outgoing.reshape(devices, capacity, width),
        ALL,
        split_axis=0,
        concat_axis=0,
        tiled=True,
    )
    back, sort, unsort, starts = pl.pallas_call(
        functools.partial(table_kernel, capacity),
        out_shape=(
            shape((tok_dev, slots)),
            shape((slots, slots)),
            shape((slots, slots)),
            shape((8, 128), jnp.int32),
        ),
        in_specs=smem(1) + vmem(2),
        out_specs=tuple(vmem(4)),
        compiler_params=params(16 * 1024 * 1024),
        cost_estimate=pl.CostEstimate(flops=40_000_000, bytes_accessed=400_000, transcendentals=0),
        name="table",
    )(me, owners, requests)
    arrived, piece, back, sort, unsort, starts = lax.optimization_barrier(
        (arrived, piece, back, sort, unsort, starts)
    )
    piece = lax.ppermute(piece, "pair", [(0, 1), (1, 0)])
    attended = pl.pallas_call(
        attend_kernel,
        out_shape=shape((slots, width)),
        in_specs=smem(2) + vmem(3) + hbm(3),
        out_specs=vmem(1)[0],
        scratch_shapes=[
            pltpu.VMEM((slots, width), jnp.bfloat16),
            pltpu.VMEM((slots, 3 * width), jnp.bfloat16),
            pltpu.VMEM((slots, width), jnp.bfloat16),
            pltpu.VMEM(w_qkv.shape, jnp.bfloat16),
            pltpu.VMEM(cache_k.shape, jnp.bfloat16),
            pltpu.VMEM(cache_v.shape, jnp.bfloat16),
            pltpu.SemaphoreType.DMA((3,)),
            pltpu.SemaphoreType.DMA((cache_k.shape[0], 2)),
        ],
        compiler_params=params(50 * 1024 * 1024),
        cost_estimate=pl.CostEstimate(
            flops=16 * slots * width * width, bytes_accessed=20_000_000, transcendentals=4_000_000
        ),
        name="attend",
    )(
        starts,
        cache_len,
        sort,
        unsort,
        arrived.reshape(slots, width),
        w_qkv,
        cache_k,
        cache_v,
    )
    attended, piece = lax.optimization_barrier((attended, piece))
    sharers = lax.axis_size("req")
    rows = w_fc1.shape[0] // sharers
    by_permutes = rows % 128 == 0 and w_fc1.shape[0] == w_fc1.shape[1]

    def from_sharer(piece, by):
        return lax.ppermute(piece, "req", [(i, i ^ by) for i in range(sharers)])

    if by_permutes:
        mate = from_sharer(piece, 1)
        shares = [from_sharer(piece, by) for by in range(2, sharers, 2)]
    else:
        pair = lax.all_gather(piece, "req", axis=0, tiled=True)
    returned = lax.all_to_all(
        attended.reshape(devices, capacity, width),
        ALL,
        split_axis=0,
        concat_axis=0,
        tiled=True,
    )
    normed = pl.pallas_call(
        out_kernel,
        out_shape=shape((tok_dev, width)),
        in_specs=vmem(6),
        out_specs=vmem(1)[0],
        compiler_params=params(16 * 1024 * 1024),
        name="out_norm",
    )(
        back,
        returned.reshape(slots, width),
        w_out,
        tokens,
        ln1_gain.reshape(1, width),
        ln1_bias.reshape(1, width),
    )
    others = lax.axis_size("other")
    cost = pl.CostEstimate(
        flops=4 * tok_dev * w_fc1.size, bytes_accessed=4 * w_fc1.size, transcendentals=0
    )

    def near_part(states):
        return pl.pallas_call(
            ffn_kernel,
            out_shape=shape(states.shape, jnp.float32),
            in_specs=vmem(3),
            out_specs=vmem(1)[0],
            compiler_params=params(16 * 1024 * 1024),
            cost_estimate=cost,
            name="ffn_near",
        )(states, w_fc1, w_fc2)

    def pair_part(states, base, dtype):
        return pl.pallas_call(
            pair_kernel,
            out_shape=shape((tok_dev, width), dtype),
            in_specs=vmem(3),
            out_specs=vmem(1)[0],
            compiler_params=params(16 * 1024 * 1024),
            cost_estimate=cost,
            name="ffn_pair",
        )(states, base, pair)

    def shift(states, by):
        return lax.ppermute(states, "other", [(i, i ^ by) for i in range(others)])

    if by_permutes:
        halves = 1
        half = tok_dev // halves
        visitors = [
            [shift(normed[i * half : (i + 1) * half], by) for i in range(halves)]
            for by in range(1, others)
        ]
        own = near_part(normed)
        shares, visitors, own = lax.optimization_barrier((shares, visitors, own))
        shares = [piece, mate] + [got for s in shares for got in (s, from_sharer(s, 1))]
        bases = [[near_part(visitor) for visitor in some] for some in visitors]
        shares, bases = lax.optimization_barrier((shares, bases))
        me_req = lax.axis_index("req").astype(jnp.int32).reshape(1)
        pair_weights = pl.pallas_call(
            assemble_kernel,
            out_shape=(shape(w_fc1.shape), shape(w_fc2.shape)),
            in_specs=smem(1) + vmem(len(shares)),
            out_specs=tuple(vmem(2)),
            scratch_shapes=[pltpu.SemaphoreType.DMA((2, len(shares)))],
            compiler_params=params(16 * 1024 * 1024),
            cost_estimate=cost,
            name="assemble",
        )(me_req, *shares)

        def whole(states, base, dtype):
            return pl.pallas_call(
                add_kernel,
                out_shape=shape(states.shape, dtype),
                in_specs=vmem(4),
                out_specs=vmem(1)[0],
                compiler_params=params(16 * 1024 * 1024),
                cost_estimate=cost,
                name="ffn_pair",
            )(states, base, *pair_weights)

        parts = []
        for by, (some, their) in enumerate(zip(visitors, bases), 1):
            for visitor, base in zip(some, their):
                parts.append(shift(whole(visitor, base, jnp.bfloat16), by))
        own = whole(normed, own, jnp.float32)
    else:
        halves = 1
        pair = pair.reshape(sharers, -1, pair.shape[1])
        visitors = [shift(normed, by) for by in range(1, others)]
        own = near_part(normed)
        visitors, own = lax.optimization_barrier((visitors, own))
        bases = [near_part(visitor) for visitor in visitors]
        bases, pair = lax.optimization_barrier((bases, pair))
        parts = [
            shift(pair_part(visitor, base, jnp.bfloat16), by)
            for by, (visitor, base) in enumerate(zip(visitors, bases), 1)
        ]
        own = pair_part(normed, own, jnp.float32)
    return pl.pallas_call(
        functools.partial(final_kernel, halves),
        out_shape=shape((tok_dev, width)),
        in_specs=vmem(len(parts) + 4),
        out_specs=vmem(1)[0],
        compiler_params=params(16 * 1024 * 1024),
        name="final_norm",
    )(ln2_gain.reshape(1, width), ln2_bias.reshape(1, width), normed, own, *parts)


def solution(mesh):
    n_req, n_mlp = mesh.devices.shape
    split = jax.sharding.Mesh(mesh.devices.reshape(n_req, n_mlp // 2, 2), ALL)
    mlp = ("other", "pair")
    placed = (
        P(ALL, None),
        P(),
        P(),
        P(ALL),
        P(ALL, None, None),
        P(ALL, None, None),
        P(),
        P(),
        P(None, mlp),
        P(mlp, None),
        P(),
        P(),
        P(),
        P(),
    )
    return jax.shard_map(
        per_device, mesh=split, in_specs=placed, out_specs=P(ALL, None), check_vma=False
    )
```
